32 devices in a mesh: tm: 8 (over z, x), space: 4 (over y, core).
Axes of the slice: x: 2, y: 2, z: 4, core: 2. Of those that a mesh axis runs over, the one named last changes fastest.
Arguments:
- snapshots: bfloat16 [256, 3, 131072], P('tm', None, 'space'), may hold values from -12 to 12
- cell_weights: float32 [131072], P('space'), may hold values from 0.2 to 5
- freq_order: int32 [32], replicated, may hold values from 0 to 31, each once
Outputs:
- energies: float32 [32, 4], P('tm')
- modes: bfloat16 [32, 4, 2, 3, 131072], P('tm', None, None, None, 'space')
The draws below stay inside these ranges and needn't reach their ends.
All inputs are finite; a program needn't handle non-finite values.
Results may differ from the reference program's by a relative error of at most 0.0043.
Values may be sent and summed in bfloat16 or wider, within the bound.
No kernel may reach another device: no remote copies, remote signals or barrier semaphores. Data moves between devices by JAX's collectives and lax.ppermute only.
A program may use at most 192 MiB of HBM per device.

```python
import math
import jax
import jax.numpy as jnp
from jax import lax

NFFT = 64
COMP = 3
MODES = 4
SWEEPS = 3
HALF = 32
NF = 32
SNAPS = 256
NB = 7
CELLS = 131072
N_TM = 8


def draw_snapshots(key, part):
    noise_key = jax.random.fold_in(jax.random.fold_in(key, 7), 0)
    rate_key = jax.random.fold_in(jax.random.fold_in(key, 7), 1)
    shape_key = jax.random.fold_in(jax.random.fold_in(key, 7), 2)
    level_key = jax.random.fold_in(jax.random.fold_in(key, 7), 4)
    time_axis = jnp.arange(SNAPS, dtype=jnp.float32)[:, None]
    base_rates = jnp.arange(NF, dtype=jnp.float32)[None, :]
    wave_rates = base_rates + jax.random.uniform(rate_key, (1, NF), jnp.float32, -0.35, 0.35)
    angle_rows = 2.0 * math.pi * wave_rates * time_axis / NFFT
    temporal = jnp.concatenate([jnp.cos(angle_rows), jnp.sin(angle_rows)], 1)
    levels = jnp.exp(jax.random.uniform(level_key, (NF,), jnp.float32, math.log(0.15), math.log(0.45)))
    level_rows = jnp.concatenate([levels, levels], 0)[:, None]
    spatial = level_rows * jax.random.normal(shape_key, (2 * NF, COMP * CELLS), jnp.float32)
    coherent = jnp.dot(temporal, spatial, precision=lax.Precision.HIGHEST).reshape(SNAPS, COMP, CELLS)
    noise_part = jax.random.normal(noise_key, (SNAPS, COMP, CELLS), jnp.float32)
    velocity = noise_part + coherent
    return jnp.clip(velocity, -12.0, 12.0).astype(jnp.bfloat16)


def block_scale(rng, extent, cuts, least, largest):
    gain, own = 1.0, jax.random.fold_in(rng, 6)
    for position, shards_of in cuts:
        steps = jnp.exp(jax.random.uniform(jax.random.fold_in(own, position), (shards_of,), jnp.float32, least / len(cuts), largest / len(cuts)))
        gain = gain * jnp.repeat(steps, extent[position] // shards_of).reshape([-1 if axis == position else 1 for axis in range(len(extent))])
    return gain


def setup_inputs(seed: int = 0) -> dict:
    splits = jax.random.split(jax.random.key(seed), 4)
    snapshots = draw_snapshots(jax.random.fold_in(splits[3], 71), 0)
    cell_weights = jnp.clip(jnp.exp(math.log(5.0) - 3.218876 * jax.random.uniform(splits[1], (CELLS,), jnp.float32) ** block_scale(splits[1], (CELLS,), ((0, 4),), -0.2, 0.2)), 0.2, 5.0)
    freq_order = jax.random.permutation(splits[2], NF).astype(jnp.int32)
    return dict(snapshots=snapshots, cell_weights=cell_weights, freq_order=freq_order)


shift_rate = 0.61
top_precision = lax.Precision.HIGHEST

def window_tables():
    sample = jnp.arange(NFFT, dtype=jnp.int32)
    freq_rows = jnp.arange(NF, dtype=jnp.int32)
    turn_index = (freq_rows[:, None] * sample[None, :] % NFFT).astype(jnp.float32)
    angle_grid = 2.0 * math.pi * turn_index / NFFT
    hann_window = 0.5 - 0.5 * jnp.cos(2.0 * math.pi * sample.astype(jnp.float32) / NFFT)
    dft_basis = jnp.stack([hann_window * jnp.cos(angle_grid), -hann_window * jnp.sin(angle_grid)], 0)
    return (dft_basis.astype(jnp.bfloat16), jnp.sum(hann_window * hann_window))

def start_vectors(block_count):
    rows_idx = jnp.arange(block_count, dtype=jnp.float32)[:, None] + 1.0
    cols_idx = jnp.arange(MODES, dtype=jnp.float32)[None, :] + 1.0
    return jnp.cos(shift_rate * rows_idx * cols_idx)

def complex_apply(real_part, imag_part, vec_re, vec_im):
    first_re = jnp.einsum('fab,fbk->fak', real_part, vec_re, precision=top_precision)
    first_im = jnp.einsum('fab,fbk->fak', imag_part, vec_im, precision=top_precision)
    cross_re = jnp.einsum('fab,fbk->fak', real_part, vec_im, precision=top_precision)
    cross_im = jnp.einsum('fab,fbk->fak', imag_part, vec_re, precision=top_precision)
    return (first_re - first_im, cross_re + cross_im)

def orthonormal(image_re, image_im):
    done_re = []
    done_im = []
    for column in range(MODES):
        col_re = image_re[:, :, column]
        col_im = image_im[:, :, column]
        for earlier in range(column):
            prev_re = done_re[earlier]
            prev_im = done_im[earlier]
            inner_re = lax.optimization_barrier(jnp.sum(prev_re * col_re + prev_im * col_im, axis=1, keepdims=True))
            inner_im = lax.optimization_barrier(jnp.sum(prev_re * col_im - prev_im * col_re, axis=1, keepdims=True))
            col_re = col_re - (inner_re * prev_re - inner_im * prev_im)
            col_im = col_im - (inner_re * prev_im + inner_im * prev_re)
        length = jnp.sqrt(lax.optimization_barrier(jnp.sum(col_re * col_re + col_im * col_im, axis=1, keepdims=True)))
        done_re.append(col_re / length)
        done_im.append(col_im / length)
    return (jnp.stack(done_re, 2), jnp.stack(done_im, 2))

def power_sweeps(real_part, imag_part):
    start_table = start_vectors(real_part.shape[-1])
    vec_re = jnp.broadcast_to(start_table, real_part.shape[:1] + start_table.shape)
    vec_im = jnp.zeros_like(vec_re)
    for sweep_step in range(SWEEPS):
        image_re, image_im = complex_apply(real_part, imag_part, vec_re, vec_im)
        vec_re, vec_im = orthonormal(image_re, image_im)
    applied_re, applied_im = complex_apply(real_part, imag_part, vec_re, vec_im)
    energy = lax.optimization_barrier(jnp.sum(vec_re * applied_re + vec_im * applied_im, axis=1))
    return (vec_re, vec_im, energy)

def mixing_rows(vec_re, vec_im, factor):
    turned_re = jnp.swapaxes(vec_re, 1, 2) * factor
    turned_im = jnp.swapaxes(vec_im, 1, 2) * factor
    real_out = jnp.stack([turned_re, -turned_im], 2)
    imag_out = jnp.stack([turned_im, turned_re], 2)
    return jnp.stack([real_out, imag_out], 2).astype(jnp.bfloat16)

def reference(snapshots, cell_weights, freq_order):
    dft_basis, energy_sum = window_tables()
    gram_scale = 1.0 / (energy_sum * (COMP * CELLS))
    factor = 1.0 / jnp.sqrt(energy_sum)
    time_rows = snapshots.reshape(N_TM, HALF, COMP * CELLS).transpose(1, 0, 2).reshape(HALF, N_TM * COMP * CELLS)
    point_weights = jnp.tile(cell_weights, COMP)

    def one_frequency(frequency):
        basis_rows = dft_basis[:, frequency, :]
        split_basis = jnp.concatenate([basis_rows[:, :HALF], basis_rows[:, HALF:]], 0)
        halves_out = jnp.dot(split_basis, time_rows, preferred_element_type=jnp.float32).reshape(4, N_TM, COMP * CELLS)
        spectra = (halves_out[0:2, :-1] + halves_out[2:4, 1:]).astype(jnp.bfloat16)
        weighted = (spectra.astype(jnp.float32) * point_weights).astype(jnp.bfloat16)
        products = jnp.dot(weighted.reshape(2 * NB, -1), spectra.reshape(2 * NB, -1).T, preferred_element_type=jnp.float32).reshape(2, NB, 2, NB)
        gram_re = (products[0, :, 0] + products[1, :, 1]) * gram_scale
        gram_im = (products[0, :, 1] - products[1, :, 0]) * gram_scale
        vec_re, vec_im, energy = power_sweeps(gram_re[None], gram_im[None])
        mixing = mixing_rows(vec_re, vec_im, factor)[0].reshape(2 * MODES, 2 * NB)
        mode_rows = jnp.dot(mixing, spectra.reshape(2 * NB, -1), preferred_element_type=jnp.float32)
        return (energy[0], mode_rows.astype(jnp.bfloat16).reshape(MODES, 2, COMP, CELLS))
    energies, modes = lax.map(one_frequency, freq_order)
    return (energies, modes)
```

```python
import functools
import math

import jax
import jax.numpy as jnp
from jax import lax
from jax.experimental import pallas as pl
from jax.experimental.pallas import tpu as pltpu
from jax.sharding import PartitionSpec as P

NFFT = 64
COMP = 3
MODES = 4
SWEEPS = 3
NF = 32

CHUNKS = ((0, 0, 2), (0, 2, 6), (0, 8, 8), (1, 0, 8), (1, 8, 8), (2, 0, 8), (2, 8, 6), (2, 14, 2))
KINDS = (0, 1, 0, 1, 0, 1, 0, 1)
PARTS = 16

shift_rate = 0.61
top_precision = lax.Precision.HIGHEST


def hann_window():
    sample = jnp.arange(NFFT, dtype=jnp.int32)
    return 0.5 - 0.5 * jnp.cos(2.0 * math.pi * sample.astype(jnp.float32) / NFFT)


def basis_rows(freqs, sines):
    sample = jnp.arange(NFFT, dtype=jnp.int32)
    turn_index = (freqs[:, None] * sample[None, :] % NFFT).astype(jnp.float32)
    angle_grid = 2.0 * math.pi * turn_index / NFFT
    window = hann_window()
    rows = jnp.where(sines[:, None], -window * jnp.sin(angle_grid), window * jnp.cos(angle_grid))
    return rows.astype(jnp.bfloat16)


def pick(values, places):
    hot = places[:, None] == jnp.arange(values.shape[0], dtype=jnp.int32)[None, :]
    return jnp.sum(jnp.where(hot, values[None, :], 0), axis=1)


def start_vectors(block_count):
    rows_idx = jnp.arange(block_count, dtype=jnp.float32)[:, None] + 1.0
    cols_idx = jnp.arange(MODES, dtype=jnp.float32)[None, :] + 1.0
    return jnp.cos(shift_rate * rows_idx * cols_idx)


def table_of(role, devices, freqs, sines):
    rows = basis_rows(freqs, sines)
    first, second = rows[:, : NFFT // 2], rows[:, NFFT // 2 :]
    low = role < devices // 2
    middle = (role == devices // 2 - 1) | (role == devices // 2)
    near = jnp.where(low, first, second)
    beside = jnp.where(middle, jnp.zeros_like(first), jnp.where(low, second, first))
    return near, beside


def beside_of(role, devices):
    if role in (devices // 2 - 1, devices // 2):
        return None
    return role + 1 if role < devices // 2 else role - 1


def transform_kernel(count, rows, table_ref, *refs):
    ins, outs = refs[:count], refs[count:]
    total = None
    for place, ref in enumerate(ins):
        data = ref[...].reshape(ref.shape[-2:])
        half = data.shape[0]
        part = jnp.dot(
            table_ref[:, place * half : (place + 1) * half], data, preferred_element_type=jnp.float32
        )
        total = part if total is None else total + part
    for place, out in enumerate(outs):
        out[...] = total[place * rows : (place + 1) * rows].astype(out.dtype)


def transform(table, own, others, comp, start, size, devices, rows, tile):
    half = own.shape[1]
    ins = [pl.BlockSpec(table.shape, lambda g: (0, 0))]
    ins.append(pl.BlockSpec((1, half, tile), lambda g: (comp, 0, start // tile + g)))
    ins += [pl.BlockSpec((half, tile), lambda g: (0, g)) for _ in others]
    return pl.pallas_call(
        functools.partial(transform_kernel, 1 + len(others), rows),
        grid=(size // tile,),
        in_specs=ins,
        out_specs=[pl.BlockSpec((rows, tile), lambda g: (0, g))] * devices,
        out_shape=[jax.ShapeDtypeStruct((rows, size), jnp.bfloat16)] * devices,
        cost_estimate=pl.CostEstimate(
            flops=2 * table.size * size, bytes_accessed=2 * size * (table.shape[0] + table.shape[1]), transcendentals=0
        ),
        name="transform",
    )(table, own, *others)


def gram_kernel(count, weight_ref, *refs):
    messages = refs[:count]
    before, store, total = refs[-4], refs[-2], refs[-1]

    @pl.when(pl.program_id(0) == 0)
    def _():
        total[...] = before[...]

    wide = jnp.concatenate([ref[...].astype(jnp.float32) for ref in messages], 0)
    spectra = wide.astype(jnp.bfloat16)
    weighted = (wide * weight_ref[...]).astype(jnp.bfloat16)
    store[...] = spectra[None]
    total[...] += lax.dot_general(
        weighted, spectra, (((1,), (1,)), ((), ())), preferred_element_type=jnp.float32
    )


def gram(messages, weights, before, held, comp, start, size, tile):
    count = len(messages)
    rows = messages[0].shape[0]
    whole = count * rows
    spot = lambda g: (comp, 0, start // tile + g)
    return pl.pallas_call(
        functools.partial(gram_kernel, count),
        grid=(size // tile,),
        in_specs=[pl.BlockSpec((1, tile), lambda g: (0, start // tile + g))]
        + [pl.BlockSpec((rows, tile), lambda g: (0, g))] * count
        + [pl.BlockSpec((whole, whole), lambda g: (0, 0))]
        + [pl.BlockSpec(memory_space=pl.ANY)],
        out_specs=[pl.BlockSpec((1, whole, tile), spot), pl.BlockSpec((whole, whole), lambda g: (0, 0))],
        out_shape=[
            jax.ShapeDtypeStruct(held.shape, held.dtype),
            jax.ShapeDtypeStruct((whole, whole), jnp.float32),
        ],
        input_output_aliases={count + 2: 0},
        cost_estimate=pl.CostEstimate(flops=2 * whole * whole * size, bytes_accessed=4 * whole * size, transcendentals=0),
        name="gram",
    )(weights, *messages, before, held)


def modes_kernel(mix_ref, held_ref, out_ref):
    rows = jnp.dot(mix_ref[...], held_ref[0], preferred_element_type=jnp.float32)
    freqs, modes = out_ref.shape[:2]
    for f in range(freqs):
        for k in range(modes):
            place = 2 * (f * modes + k)
            out_ref[f, k, 0] = rows[place : place + 2].astype(out_ref.dtype)


def modes_of(mix, held, freqs, tile):
    comps, whole, cells = held.shape
    return pl.pallas_call(
        modes_kernel,
        grid=(comps, cells // tile),
        in_specs=[
            pl.BlockSpec(mix.shape, lambda c, g: (0, 0)),
            pl.BlockSpec((1, whole, tile), lambda c, g: (c, 0, g)),
        ],
        out_specs=pl.BlockSpec((freqs, MODES, 1, 2, tile), lambda c, g: (0, 0, c, 0, g)),
        out_shape=jax.ShapeDtypeStruct((freqs, MODES, comps, 2, cells), jnp.bfloat16),
        name="modes",
    )(mix, held)


def blank_kernel(out_ref):
    pass


def blank(shape, dtype):
    return pl.pallas_call(
        blank_kernel,
        out_specs=pl.BlockSpec(memory_space=pl.ANY),
        out_shape=jax.ShapeDtypeStruct(shape, dtype),
        name="blank",
    )()


def complex_apply(real_part, imag_part, vec_re, vec_im):
    first_re = jnp.einsum("fab,fbk->fak", real_part, vec_re, precision=top_precision)
    first_im = jnp.einsum("fab,fbk->fak", imag_part, vec_im, precision=top_precision)
    cross_re = jnp.einsum("fab,fbk->fak", real_part, vec_im, precision=top_precision)
    cross_im = jnp.einsum("fab,fbk->fak", imag_part, vec_re, precision=top_precision)
    return (first_re - first_im, cross_re + cross_im)


def orthonormal(image_re, image_im):
    done_re = []
    done_im = []
    for column in range(MODES):
        col_re = image_re[:, :, column]
        col_im = image_im[:, :, column]
        for earlier in range(column):
            prev_re = done_re[earlier]
            prev_im = done_im[earlier]
            inner_re = jnp.sum(prev_re * col_re + prev_im * col_im, axis=1, keepdims=True)
            inner_im = jnp.sum(prev_re * col_im - prev_im * col_re, axis=1, keepdims=True)
            col_re = col_re - (inner_re * prev_re - inner_im * prev_im)
            col_im = col_im - (inner_re * prev_im + inner_im * prev_re)
        length = jnp.sqrt(jnp.sum(col_re * col_re + col_im * col_im, axis=1, keepdims=True))
        done_re.append(col_re / length)
        done_im.append(col_im / length)
    return (jnp.stack(done_re, 2), jnp.stack(done_im, 2))


def power_sweeps(real_part, imag_part):
    start_table = start_vectors(real_part.shape[-1])
    vec_re = jnp.broadcast_to(start_table, real_part.shape[:1] + start_table.shape)
    vec_im = jnp.zeros_like(vec_re)
    for sweep_step in range(SWEEPS):
        image_re, image_im = complex_apply(real_part, imag_part, vec_re, vec_im)
        vec_re, vec_im = orthonormal(image_re, image_im)
    applied_re, applied_im = complex_apply(real_part, imag_part, vec_re, vec_im)
    energy = jnp.sum(vec_re * applied_re + vec_im * applied_im, axis=1)
    return (vec_re, vec_im, energy)


def mixing_rows(vec_re, vec_im, factor):
    turned_re = jnp.swapaxes(vec_re, 1, 2) * factor
    turned_im = jnp.swapaxes(vec_im, 1, 2) * factor
    real_out = jnp.stack([turned_re, -turned_im], 2)
    imag_out = jnp.stack([turned_im, turned_re], 2)
    return jnp.stack([real_out, imag_out], 2)


def per_device(snapshots, cell_weights, freq_order):
    devices = lax.axis_size("tm")
    spaces = lax.axis_size("space")
    me = lax.axis_index("tm")
    half, comps, cells = snapshots.shape
    freqs = NF // devices
    rows = 2 * freqs
    unit = cells // PARTS
    window = hann_window()
    energy_sum = jnp.sum(window * window)
    gram_scale = 1.0 / (energy_sum * (comps * cells * spaces))
    factor = 1.0 / jnp.sqrt(energy_sum)

    own = jnp.transpose(snapshots, (1, 0, 2))
    weights = cell_weights.reshape(1, cells)

    line = jnp.arange(devices * rows, dtype=jnp.int32)
    target = jnp.bitwise_xor(me, line // rows)
    line_freq = pick(freq_order, target * freqs + line % rows // 2)
    line_sine = line % 2 == 1
    near, beside = table_of(me, devices, line_freq, line_sine)
    table_0 = jnp.concatenate([near, beside], 1)
    near, beside = table_of(jnp.bitwise_xor(me, 1), devices, line_freq, line_sine)
    odd = me % 2 == 1
    own_beside = jnp.where(me < devices // 2, odd, ~odd)
    nothing = jnp.zeros_like(beside)
    table_1 = jnp.concatenate(
        [jnp.where(own_beside, beside, nothing), near, jnp.where(own_beside, nothing, beside)], 1
    )
    pairs_0 = []
    pairs_1 = []
    for device in range(devices):
        source = beside_of(device, devices)
        if source is not None:
            pairs_0.append((source, device))
        source = beside_of(device ^ 1, devices)
        if source is not None and source != device:
            pairs_1.append((source, device))
    swap = [(device, device ^ 1) for device in range(devices)]

    total = jnp.zeros((devices * rows, devices * rows), jnp.float32)
    held = blank((comps, devices * rows, cells), jnp.bfloat16)
    for (comp, first, length), kind in zip(CHUNKS, KINDS):
        start, size = first * unit, length * unit
        piece = own[comp, :, start : start + size]
        if kind == 0:
            table, others = table_0, [lax.ppermute(piece, "tm", pairs_0)]
        else:
            table, others = table_1, [lax.ppermute(piece, "tm", swap), lax.ppermute(piece, "tm", pairs_1)]
        messages = transform(table, own, others, comp, start, size, devices, rows, unit)
        landed = [None] * devices
        across = list(range(devices // 2, devices))
        inside = list(range(1, devices // 2)) + [0]
        for place in [p for pair in zip(across, inside) for p in pair]:
            landed[place ^ kind] = (
                messages[0]
                if place == 0
                else lax.ppermute(messages[place], "tm", [(d, d ^ place) for d in range(devices)])
            )
        held, total = gram(landed, weights, total, held, comp, start, size, unit)
    step = 1
    while step < spaces:
        total = total + lax.ppermute(total, "space", [(d, d ^ step) for d in range(spaces)])
        step *= 2

    slot = jnp.arange(devices, dtype=jnp.int32)
    role = jnp.bitwise_xor(me, slot)
    block = jnp.where(role < devices // 2, role, role - 1)
    to_block = (block[None, :] == jnp.arange(devices - 1, dtype=jnp.int32)[:, None]).astype(jnp.float32)
    products = total.reshape(devices, freqs, 2, devices, freqs, 2)
    same = jnp.eye(freqs, dtype=jnp.float32)[None, :, None, None, :, None]
    products = jnp.sum(products * same, axis=4)
    products = jnp.einsum(
        "ai,ifrjs,bj->frasb", to_block, products, to_block, precision=top_precision
    )
    gram_re = products[:, 0, :, 0, :] + products[:, 1, :, 1, :]
    gram_im = products[:, 0, :, 1, :] - products[:, 1, :, 0, :]
    vec_re, vec_im, energies = power_sweeps(gram_re * gram_scale, gram_im * gram_scale)
    mixing = mixing_rows(vec_re, vec_im, factor)
    spread = jnp.einsum("fkorb,bi->fkoir", mixing, to_block, precision=top_precision)
    eye = jnp.eye(freqs, dtype=jnp.float32)
    mix = spread[:, :, :, :, None, :] * eye[:, None, None, None, :, None]
    mix = mix.reshape(freqs * MODES * 2, devices * rows).astype(jnp.bfloat16)
    out = modes_of(mix, held, freqs, cells // 8)
    return (energies, jnp.transpose(out, (0, 1, 3, 2, 4)))


def solution(mesh):
    return jax.shard_map(
        per_device,
        mesh=mesh,
        in_specs=(P("tm", None, "space"), P("space"), P()),
        out_specs=(P("tm", None), P("tm", None, None, None, "space")),
        check_vma=False,
    )
```

```python
import functools
import math

import jax
import jax.numpy as jnp
from jax import lax
from jax.experimental import pallas as pl
from jax.experimental.pallas import tpu as pltpu
from jax.sharding import PartitionSpec as P

NFFT = 64
HALF = NFFT // 2
MODES = 4
SWEEPS = 3
NF = 32
GROUPS = 2
PER_GROUP = NF // GROUPS

CHUNKS_IN = ((0, 0, 4), (1, 0, 4), (2, 0, 2), (2, 2, 2))
CHUNKS_OUT = (2, 0, 1, 3)
QUARTERS = 4

shift_rate = 0.61
BIG = 48 * 1024 * 1024


def hann_window():
    sample = jnp.arange(NFFT, dtype=jnp.int32)
    return 0.5 - 0.5 * jnp.cos(2.0 * math.pi * sample.astype(jnp.float32) / NFFT)


def window_basis(freqs):
    sample = jnp.arange(NFFT, dtype=jnp.int32)
    turn_index = (freqs[:, None] * sample[None, :] % NFFT).astype(jnp.float32)
    angle_grid = 2.0 * math.pi * turn_index / NFFT
    window = hann_window()
    return jnp.stack([window * jnp.cos(angle_grid), -window * jnp.sin(angle_grid)], 0).astype(jnp.bfloat16)


def band_table(freq_order, me, devices):
    basis = window_basis(freq_order).reshape(2, GROUPS, PER_GROUP, NFFT)
    basis = jnp.transpose(basis, (1, 0, 2, 3))
    half_of = jnp.bitwise_xor(me, jnp.arange(devices, dtype=jnp.int32))
    block = jnp.arange(devices - 1, dtype=jnp.int32)
    first = (half_of[None, :] == block[:, None])[None, :, None, None, :, None]
    second = (half_of[None, :] == block[:, None] + 1)[None, :, None, None, :, None]
    low = basis[:, None, :, :, None, :HALF]
    high = basis[:, None, :, :, None, HALF:]
    nothing = jnp.zeros((), jnp.bfloat16)
    band = jnp.where(first, low, jnp.where(second, high, nothing))
    return band.reshape(GROUPS, (devices - 1) * 2 * PER_GROUP, devices * HALF)


def pick_kernel(count, comp, start, size, sub, me_ref, own_ref, *refs):
    outs, sems = refs[-count - 1 : -1], refs[-1]
    me = me_ref[0]
    copies = []
    for place in range(count):
        there = pl.multiple_of(jnp.bitwise_xor(me, place + 1) * sub + start, 128)
        copies.append(
            pltpu.make_async_copy(own_ref.at[comp, :, pl.ds(there, size)], outs[place], sems.at[place])
        )
    for copy in copies:
        copy.start()
    for copy in copies:
        copy.wait()


def pick(me, own, after, devices, comp, start, size, sub):
    count = devices - 1
    return pl.pallas_call(
        functools.partial(pick_kernel, count, comp, start, size, sub),
        in_specs=[pl.BlockSpec(memory_space=pltpu.SMEM)] + [pl.BlockSpec(memory_space=pl.ANY)] * (1 + len(after)),
        out_specs=[pl.BlockSpec(memory_space=pl.ANY)] * count,
        out_shape=[jax.ShapeDtypeStruct((own.shape[1], size), own.dtype)] * count,
        scratch_shapes=[pltpu.SemaphoreType.DMA((count,))],
        name="pick",
    )(me, own, *after)


def gather_kernel(count, me_ref, band_ref, fold_ref, weight_ref, own_ref, *refs):
    landed = refs[:count]
    before_ref, spectra_ref, total_ref, sums = refs[count:]
    step = pl.program_id(0)

    @pl.when(step == 0)
    def _():
        sums[...] = jnp.zeros_like(sums)

    data = jnp.concatenate([own_ref[0]] + [ref[...] for ref in landed], 0)
    weight = weight_ref[...]
    for group in range(GROUPS):
        wide = jnp.dot(band_ref[group], data, preferred_element_type=jnp.float32)
        spectra = wide.astype(jnp.bfloat16)
        spectra_ref[group] = spectra
        weighted = (spectra.astype(jnp.float32) * weight).astype(jnp.bfloat16)
        sums[group] += lax.dot_general(
            weighted, spectra, (((1,), (1,)), ((), ())), preferred_element_type=jnp.float32
        )

    @pl.when(step == pl.num_programs(0) - 1)
    def _():
        rows = sums.shape[1]
        line = lax.broadcasted_iota(jnp.int32, (rows, rows), 0) % PER_GROUP
        column = lax.broadcasted_iota(jnp.int32, (rows, rows), 1) % PER_GROUP
        for group in range(GROUPS):
            kept = jnp.where(line == column, sums[group], 0.0)
            total_ref[group] = before_ref[group] + jnp.dot(
                fold_ref[...], kept, precision=lax.Precision.HIGHEST, preferred_element_type=jnp.float32
            )


def gather(me, band, fold, weights, own, landed, before, comp, start, size, sub, tile):
    count = len(landed)
    half = own.shape[1]
    rows = band.shape[1]
    whole = lambda shape: pl.BlockSpec(shape, lambda g, m: (0,) * len(shape))
    spot = lambda g, m: m[0] * (sub // tile) + start // tile + g
    return pl.pallas_call(
        functools.partial(gather_kernel, count),
        grid_spec=pltpu.PrefetchScalarGridSpec(
            num_scalar_prefetch=1,
            grid=(size // tile,),
            in_specs=[
                whole(band.shape),
                whole(fold.shape),
                pl.BlockSpec((1, tile), lambda g, m: (0, spot(g, m))),
                pl.BlockSpec((1, half, tile), lambda g, m: (comp, 0, spot(g, m))),
            ]
            + [pl.BlockSpec((half, tile), lambda g, m: (0, g))] * count
            + [whole(before.shape)],
            out_specs=[pl.BlockSpec((GROUPS, rows, tile), lambda g, m: (0, 0, g)), whole(before.shape)],
            scratch_shapes=[pltpu.VMEM((GROUPS, rows, rows), jnp.float32)],
        ),
        out_shape=[
            jax.ShapeDtypeStruct((GROUPS, rows, size), jnp.bfloat16),
            jax.ShapeDtypeStruct(before.shape, jnp.float32),
        ],
        compiler_params=pltpu.CompilerParams(vmem_limit_bytes=BIG),
        cost_estimate=pl.CostEstimate(
            flops=2 * GROUPS * size * rows * (band.shape[2] + rows), bytes_accessed=2 * size * (2 * rows + 256), transcendentals=0
        ),
        name="gather",
    )(me, band, fold, weights, own, *landed, before)


def solve_kernel(blocks, me_ref, scale_ref, sums_ref, start_ref, tile_ref, mix_ref, energy_ref):
    devices = mix_ref.shape[0]
    freqs = mix_ref.shape[1] // (2 * MODES)
    padded = sums_ref.shape[1] // 2
    gram_scale = scale_ref[0]
    factor = scale_ref[1]

    def lanes(block, part):
        place = (2 * block + part) * PER_GROUP
        return jnp.concatenate([sums_ref[g, :, place : place + PER_GROUP] for g in range(GROUPS)], 1)

    real, imag = [], []
    for block in range(blocks):
        cosine, sine = lanes(block, 0), lanes(block, 1)
        real.append((cosine[:padded] + sine[padded:]) * gram_scale)
        imag.append((sine[:padded] - cosine[padded:]) * gram_scale)

    def apply(vec_re, vec_im):
        out_re = jnp.zeros((padded, NF), jnp.float32)
        out_im = out_re
        for block in range(blocks):
            at_re = vec_re[block : block + 1]
            at_im = vec_im[block : block + 1]
            out_re = out_re + (real[block] * at_re - imag[block] * at_im)
            out_im = out_im + (real[block] * at_im + imag[block] * at_re)
        return out_re, out_im

    def inner(value):
        return jnp.sum(value, axis=0, keepdims=True)

    vectors = [(start_ref[k], jnp.zeros((padded, NF), jnp.float32)) for k in range(MODES)]
    for sweep in range(SWEEPS):
        images = [apply(*vector) for vector in vectors]
        vectors = []
        for col_re, col_im in images:
            for prev_re, prev_im in vectors:
                inner_re = inner(prev_re * col_re + prev_im * col_im)
                inner_im = inner(prev_re * col_im - prev_im * col_re)
                col_re, col_im = (
                    col_re - (inner_re * prev_re - inner_im * prev_im),
                    col_im - (inner_re * prev_im + inner_im * prev_re),
                )
            length = jnp.sqrt(inner(col_re * col_re + col_im * col_im))
            vectors.append((col_re / length, col_im / length))
    for k, (vec_re, vec_im) in enumerate(vectors):
        applied_re, applied_im = apply(vec_re, vec_im)
        energy_ref[k : k + 1] = inner(vec_re * applied_re + vec_im * applied_im)

    straight, turned = [], []
    for vec_re, vec_im in vectors:
        straight += [vec_re * factor, vec_im * factor]
        turned += [-vec_im * factor, vec_re * factor]
    straight = jnp.concatenate(straight, 0).astype(jnp.bfloat16)
    turned = jnp.concatenate(turned, 0).astype(jnp.bfloat16)
    rows = tile_ref.shape[2]
    place = lax.broadcasted_iota(jnp.int32, (2 * MODES, padded, rows), 2)
    mine = place // (2 * PER_GROUP) == lax.broadcasted_iota(jnp.int32, (2 * MODES, padded, rows), 1)
    lane = lax.broadcasted_iota(jnp.int32, (2 * MODES, rows), 1)
    cosine = lane // PER_GROUP % 2 == 0
    me = me_ref[0]

    def spread(value, group):
        wide = jnp.dot(value, tile_ref[group], preferred_element_type=jnp.float32)
        wide = wide.reshape(2 * MODES, padded, rows)
        return jnp.sum(jnp.where(mine, wide, 0.0), axis=1)

    for group in range(GROUPS):
        both = jnp.where(cosine, spread(straight, group), spread(turned, group))
        for near in range(devices // GROUPS):
            device = group * (devices // GROUPS) + near
            pieces = [
                jnp.where(lane % PER_GROUP == near * freqs + f, both, 0.0) for f in range(freqs)
            ]
            mix_ref[jnp.bitwise_xor(me, device)] = jnp.concatenate(pieces, 0).astype(jnp.bfloat16)


def solve(me, scales, sums, start, tiles, devices):
    freqs = NF // devices
    rows = sums.shape[2]
    return pl.pallas_call(
        functools.partial(solve_kernel, devices - 1),
        in_specs=[pl.BlockSpec(memory_space=pltpu.SMEM)] * 2 + [pl.BlockSpec(memory_space=pltpu.VMEM)] * 3,
        out_specs=[pl.BlockSpec(memory_space=pltpu.VMEM)] * 2,
        out_shape=[
            jax.ShapeDtypeStruct((devices, freqs * MODES * 2, rows), jnp.bfloat16),
            jax.ShapeDtypeStruct((MODES, NF), jnp.float32),
        ],
        compiler_params=pltpu.CompilerParams(vmem_limit_bytes=BIG),
        name="solve",
    )(me, scales, sums, start, tiles)


def modes_kernel(me_ref, mix_ref, spectra_ref, *outs):
    devices = mix_ref.shape[0]
    part = devices // GROUPS
    freqs = outs[0].shape[0]
    per = freqs * MODES * 2
    side = me_ref[0] // part
    for h in range(GROUPS):
        mix = mix_ref[h * part : (h + 1) * part].reshape(part * per, mix_ref.shape[2])
        wide = jnp.dot(mix, spectra_ref[jnp.bitwise_xor(side, h)], preferred_element_type=jnp.float32)
        for near in range(part):
            out = outs[h * part + near]
            for f in range(freqs):
                for k in range(MODES):
                    place = near * per + 2 * (f * MODES + k)
                    out[f, k] = wide[place : place + 2].astype(out.dtype)


def modes_of(me, mix, spectra, devices, tile):
    freqs = NF // devices
    groups, rows, size = spectra.shape
    return pl.pallas_call(
        modes_kernel,
        grid_spec=pltpu.PrefetchScalarGridSpec(
            num_scalar_prefetch=1,
            grid=(size // tile,),
            in_specs=[
                pl.BlockSpec(mix.shape, lambda g, m: (0, 0, 0)),
                pl.BlockSpec((groups, rows, tile), lambda g, m: (0, 0, g)),
            ],
            out_specs=[pl.BlockSpec((freqs, MODES, 2, tile), lambda g, m: (0, 0, 0, g))] * devices,
        ),
        out_shape=[jax.ShapeDtypeStruct((freqs, MODES, 2, size), jnp.bfloat16)] * devices,
        compiler_params=pltpu.CompilerParams(vmem_limit_bytes=BIG),
        name="modes",
    )(me, mix, spectra)


def place_kernel(count, comp, start, size, sub, me_ref, *refs):
    pieces, out_ref, sems = refs[:count], refs[-2], refs[-1]
    me = me_ref[0]
    copies = []
    for place in range(count):
        there = pl.multiple_of(jnp.bitwise_xor(me, place) * sub + start, 128)
        copies.append(
            pltpu.make_async_copy(pieces[place], out_ref.at[:, :, comp, :, pl.ds(there, size)], sems.at[place])
        )
    for copy in copies:
        copy.start()
    for copy in copies:
        copy.wait()


def place(me, pieces, out, comp, start, size, sub, shape):
    count = len(pieces)
    more = [] if out is None else [out]
    return pl.pallas_call(
        functools.partial(place_kernel, count, comp, start, size, sub),
        in_specs=[pl.BlockSpec(memory_space=pltpu.SMEM)]
        + [pl.BlockSpec(memory_space=pl.ANY)] * (count + len(more)),
        out_specs=pl.BlockSpec(memory_space=pl.ANY),
        out_shape=jax.ShapeDtypeStruct(shape, jnp.bfloat16),
        input_output_aliases={count + 1: 0} if more else {},
        scratch_shapes=[pltpu.SemaphoreType.DMA((count,))],
        name="place",
    )(me, *pieces, *more)


def exchange(pieces, devices):
    landed = [None] * (devices - 1)
    across = list(range(devices // 2, devices))
    inside = list(range(1, devices // 2)) + [0]
    for step in [s for pair in zip(across, inside) for s in pair]:
        if step:
            landed[step - 1] = lax.ppermute(pieces[step - 1], "tm", [(d, d ^ step) for d in range(devices)])
    return landed


def sum_over(value, axis):
    count = lax.axis_size(axis)
    step = 1
    while step < count:
        value = value + lax.ppermute(value, axis, [(d, d ^ step) for d in range(count)])
        step *= 2
    return value


def per_device(snapshots, cell_weights, freq_order):
    devices = lax.axis_size("tm")
    spaces = lax.axis_size("space")
    index = lax.axis_index("tm")
    me = index.astype(jnp.int32).reshape(1)
    half, comps, cells = snapshots.shape
    freqs = NF // devices
    blocks = devices - 1
    padded = -(-blocks // 8) * 8
    rows = blocks * 2 * PER_GROUP
    sub = cells // devices
    unit = sub // QUARTERS
    window = hann_window()
    energy_sum = jnp.sum(window * window)
    scales = jnp.stack([1.0 / (energy_sum * (comps * cells * spaces)), 1.0 / jnp.sqrt(energy_sum)])

    own = jnp.transpose(snapshots, (1, 0, 2))
    weights = cell_weights.reshape(1, cells)
    band = band_table(freq_order, index.astype(jnp.int32), devices)
    line = jnp.arange(rows, dtype=jnp.int32)
    target = line // PER_GROUP % 2 * padded + line // (2 * PER_GROUP)
    fold = (target[None, :] == jnp.arange(2 * padded, dtype=jnp.int32)[:, None]).astype(jnp.float32)
    freq_line = jnp.arange(NF, dtype=jnp.int32)
    tiles = jnp.stack(
        [freq_line[:, None] == g * PER_GROUP + line[None, :] % PER_GROUP for g in range(GROUPS)]
    ).astype(jnp.bfloat16)
    count_a = jnp.arange(padded, dtype=jnp.float32) + 1.0
    count_k = jnp.arange(MODES, dtype=jnp.float32) + 1.0
    start_table = jnp.cos(shift_rate * count_a[None, :] * count_k[:, None])
    start_table = jnp.where(jnp.arange(padded)[None, :] < blocks, start_table, 0.0)
    start_table = jnp.broadcast_to(start_table[:, :, None], (MODES, padded, NF))

    sums = jnp.zeros((GROUPS, 2 * padded, rows), jnp.float32)
    spectra = []
    history = []
    for comp, first, length in CHUNKS_IN:
        start, size = first * unit, length * unit
        pieces = pick(me, own, history[-2:-1], devices, comp, start, size, sub)
        landed = exchange(pieces, devices)
        made, sums = gather(me, band, fold, weights, own, landed, sums, comp, start, size, sub, unit)
        spectra.append(made)
        history.append(sums)
    sums = sum_over(sum_over(sums, "space"), "tm")
    mix, energies = solve(me, scales, sums, start_table, tiles, devices)
    out = None
    shape = (freqs, MODES, comps, 2, cells)
    for chunk in CHUNKS_OUT:
        comp, first, length = CHUNKS_IN[chunk]
        made = modes_of(me, mix, spectra[chunk], devices, unit)
        landed = [made[0]] + exchange(made[1:], devices)
        out = place(me, landed, out, comp, first * unit, length * unit, sub, shape)
    mine = lax.dynamic_slice_in_dim(energies, index * freqs, freqs, 1)
    return (jnp.transpose(mine), jnp.transpose(out, (0, 1, 3, 2, 4)))


def solution(mesh):
    return jax.shard_map(
        per_device,
        mesh=mesh,
        in_specs=(P("tm", None, "space"), P("space"), P()),
        out_specs=(P("tm", None), P("tm", None, None, None, "space")),
        check_vma=False,
    )
```

```python
import functools
import math

import jax
import jax.numpy as jnp
from jax import lax
from jax.experimental import pallas as pl
from jax.experimental.pallas import tpu as pltpu
from jax.sharding import PartitionSpec as P

NFFT = 64
HALF = NFFT // 2
MODES = 4
SWEEPS = 3
NF = 32
GROUPS = 2
PER_GROUP = NF // GROUPS

CHUNKS_IN = ((0, 0, 4), (1, 0, 4), (2, 0, 2), (2, 2, 2))
CHUNKS_OUT = (2, 0, 1, 3)
QUARTERS = 4

shift_rate = 0.61
SMALL = 8 * 1024 * 1024
BIG = 32 * 1024 * 1024


def hann_window():
    sample = jnp.arange(NFFT, dtype=jnp.int32)
    return 0.5 - 0.5 * jnp.cos(2.0 * math.pi * sample.astype(jnp.float32) / NFFT)


def window_basis(freqs):
    sample = jnp.arange(NFFT, dtype=jnp.int32)
    turn_index = (freqs[:, None] * sample[None, :] % NFFT).astype(jnp.float32)
    angle_grid = 2.0 * math.pi * turn_index / NFFT
    window = hann_window()
    return jnp.stack([window * jnp.cos(angle_grid), -window * jnp.sin(angle_grid)], 0).astype(jnp.bfloat16)


def band_table(freq_order, me, devices):
    basis = window_basis(freq_order).reshape(2, GROUPS, PER_GROUP, NFFT)
    basis = jnp.transpose(basis, (1, 0, 2, 3))
    half_of = jnp.bitwise_xor(me, jnp.arange(devices, dtype=jnp.int32))
    block = jnp.arange(devices - 1, dtype=jnp.int32)
    first = (half_of[None, :] == block[:, None])[None, :, None, None, :, None]
    second = (half_of[None, :] == block[:, None] + 1)[None, :, None, None, :, None]
    low = basis[:, None, :, :, None, :HALF]
    high = basis[:, None, :, :, None, HALF:]
    nothing = jnp.zeros((), jnp.bfloat16)
    band = jnp.where(first, low, jnp.where(second, high, nothing))
    return band.reshape(GROUPS, (devices - 1) * 2 * PER_GROUP, devices * HALF)


def pick_kernel(count, comp, start, size, sub, me_ref, own_ref, *refs):
    outs, sems = refs[-count - 1 : -1], refs[-1]
    me = me_ref[0]
    copies = []
    for place in range(count):
        there = pl.multiple_of(jnp.bitwise_xor(me, place + 1) * sub + start, 128)
        copies.append(
            pltpu.make_async_copy(own_ref.at[comp, :, pl.ds(there, size)], outs[place], sems.at[place])
        )
    for copy in copies:
        copy.start()
    for copy in copies:
        copy.wait()


def pick(me, own, after, devices, comp, start, size, sub):
    count = devices - 1
    return pl.pallas_call(
        functools.partial(pick_kernel, count, comp, start, size, sub),
        in_specs=[pl.BlockSpec(memory_space=pltpu.SMEM)] + [pl.BlockSpec(memory_space=pl.ANY)] * (1 + len(after)),
        out_specs=[pl.BlockSpec(memory_space=pltpu.VMEM)] * count,
        out_shape=[jax.ShapeDtypeStruct((own.shape[1], size), own.dtype)] * count,
        scratch_shapes=[pltpu.SemaphoreType.DMA((count,))],
        compiler_params=pltpu.CompilerParams(vmem_limit_bytes=SMALL),
        name="pick",
    )(me, own, *after)


def gather_kernel(count, me_ref, band_ref, fold_ref, weight_ref, own_ref, *refs):
    landed = refs[:count]
    before_ref, spectra_ref, total_ref, sums = refs[count:]
    step = pl.program_id(0)

    @pl.when(step == 0)
    def _():
        sums[...] = jnp.zeros_like(sums)

    data = jnp.concatenate([own_ref[0]] + [ref[...] for ref in landed], 0)
    weight = weight_ref[...]
    for group in range(GROUPS):
        wide = jnp.dot(band_ref[group], data, preferred_element_type=jnp.float32)
        spectra = wide.astype(jnp.bfloat16)
        spectra_ref[group] = spectra
        weighted = (spectra.astype(jnp.float32) * weight).astype(jnp.bfloat16)
        sums[group] += lax.dot_general(
            weighted, spectra, (((1,), (1,)), ((), ())), preferred_element_type=jnp.float32
        )

    @pl.when(step == pl.num_programs(0) - 1)
    def _():
        rows = sums.shape[1]
        line = lax.broadcasted_iota(jnp.int32, (rows, rows), 0) % PER_GROUP
        column = lax.broadcasted_iota(jnp.int32, (rows, rows), 1) % PER_GROUP
        for group in range(GROUPS):
            kept = jnp.where(line == column, sums[group], 0.0)
            total_ref[group] = before_ref[group] + jnp.dot(
                fold_ref[...], kept, precision=lax.Precision.HIGHEST, preferred_element_type=jnp.float32
            )


def gather(me, band, fold, weights, own, landed, before, comp, start, size, sub, tile):
    count = len(landed)
    half = own.shape[1]
    rows = band.shape[1]
    whole = lambda shape: pl.BlockSpec(shape, lambda g, m: (0,) * len(shape))
    spot = lambda g, m: m[0] * (sub // tile) + start // tile + g
    return pl.pallas_call(
        functools.partial(gather_kernel, count),
        grid_spec=pltpu.PrefetchScalarGridSpec(
            num_scalar_prefetch=1,
            grid=(size // tile,),
            in_specs=[
                whole(band.shape),
                whole(fold.shape),
                pl.BlockSpec((1, tile), lambda g, m: (0, spot(g, m))),
                pl.BlockSpec((1, half, tile), lambda g, m: (comp, 0, spot(g, m))),
            ]
            + [pl.BlockSpec((half, tile), lambda g, m: (0, g))] * count
            + [whole(before.shape)],
            out_specs=[pl.BlockSpec((GROUPS, rows, tile), lambda g, m: (0, 0, g)), whole(before.shape)],
            scratch_shapes=[pltpu.VMEM((GROUPS, rows, rows), jnp.float32)],
        ),
        out_shape=[
            jax.ShapeDtypeStruct((GROUPS, rows, size), jnp.bfloat16),
            jax.ShapeDtypeStruct(before.shape, jnp.float32),
        ],
        compiler_params=pltpu.CompilerParams(vmem_limit_bytes=BIG),
        cost_estimate=pl.CostEstimate(
            flops=2 * GROUPS * size * rows * (band.shape[2] + rows), bytes_accessed=2 * size * (2 * rows + 256), transcendentals=0
        ),
        name="gather",
    )(me, band, fold, weights, own, *landed, before)


def solve_kernel(blocks, me_ref, scale_ref, sums_ref, start_ref, tile_ref, mix_ref, energy_ref):
    devices = mix_ref.shape[0]
    freqs = mix_ref.shape[1] // (2 * MODES)
    padded = sums_ref.shape[1] // 2
    gram_scale = scale_ref[0]
    factor = scale_ref[1]

    def lanes(block, part):
        place = (2 * block + part) * PER_GROUP
        return jnp.concatenate([sums_ref[g, :, place : place + PER_GROUP] for g in range(GROUPS)], 1)

    real, imag = [], []
    for block in range(blocks):
        cosine, sine = lanes(block, 0), lanes(block, 1)
        real.append((cosine[:padded] + sine[padded:]) * gram_scale)
        imag.append((sine[:padded] - cosine[padded:]) * gram_scale)

    def apply(vec_re, vec_im):
        out_re = jnp.zeros((padded, NF), jnp.float32)
        out_im = out_re
        for block in range(blocks):
            at_re = vec_re[block : block + 1]
            at_im = vec_im[block : block + 1]
            out_re = out_re + (real[block] * at_re - imag[block] * at_im)
            out_im = out_im + (real[block] * at_im + imag[block] * at_re)
        return out_re, out_im

    def inner(value):
        return jnp.sum(value, axis=0, keepdims=True)

    vectors = [(start_ref[k], jnp.zeros((padded, NF), jnp.float32)) for k in range(MODES)]
    for sweep in range(SWEEPS):
        images = [apply(*vector) for vector in vectors]
        vectors = []
        for col_re, col_im in images:
            for prev_re, prev_im in vectors:
                inner_re = inner(prev_re * col_re + prev_im * col_im)
                inner_im = inner(prev_re * col_im - prev_im * col_re)
                col_re, col_im = (
                    col_re - (inner_re * prev_re - inner_im * prev_im),
                    col_im - (inner_re * prev_im + inner_im * prev_re),
                )
            length = jnp.sqrt(inner(col_re * col_re + col_im * col_im))
            vectors.append((col_re / length, col_im / length))
    for k, (vec_re, vec_im) in enumerate(vectors):
        applied_re, applied_im = apply(vec_re, vec_im)
        energy_ref[k : k + 1] = inner(vec_re * applied_re + vec_im * applied_im)

    straight, turned = [], []
    for vec_re, vec_im in vectors:
        straight += [vec_re * factor, vec_im * factor]
        turned += [-vec_im * factor, vec_re * factor]
    straight = jnp.concatenate(straight, 0).astype(jnp.bfloat16)
    turned = jnp.concatenate(turned, 0).astype(jnp.bfloat16)
    rows = tile_ref.shape[2]
    place = lax.broadcasted_iota(jnp.int32, (2 * MODES, padded, rows), 2)
    mine = place // (2 * PER_GROUP) == lax.broadcasted_iota(jnp.int32, (2 * MODES, padded, rows), 1)
    lane = lax.broadcasted_iota(jnp.int32, (2 * MODES, rows), 1)
    cosine = lane // PER_GROUP % 2 == 0
    me = me_ref[0]

    def spread(value, group):
        wide = jnp.dot(value, tile_ref[group], preferred_element_type=jnp.float32)
        wide = wide.reshape(2 * MODES, padded, rows)
        return jnp.sum(jnp.where(mine, wide, 0.0), axis=1)

    for group in range(GROUPS):
        both = jnp.where(cosine, spread(straight, group), spread(turned, group))
        for near in range(devices // GROUPS):
            device = group * (devices // GROUPS) + near
            pieces = [
                jnp.where(lane % PER_GROUP == near * freqs + f, both, 0.0) for f in range(freqs)
            ]
            mix_ref[jnp.bitwise_xor(me, device)] = jnp.concatenate(pieces, 0).astype(jnp.bfloat16)


def solve(me, scales, sums, start, tiles, devices):
    freqs = NF // devices
    rows = sums.shape[2]
    return pl.pallas_call(
        functools.partial(solve_kernel, devices - 1),
        in_specs=[pl.BlockSpec(memory_space=pltpu.SMEM)] * 2 + [pl.BlockSpec(memory_space=pltpu.VMEM)] * 3,
        out_specs=[pl.BlockSpec(memory_space=pltpu.VMEM)] * 2,
        out_shape=[
            jax.ShapeDtypeStruct((devices, freqs * MODES * 2, rows), jnp.bfloat16),
            jax.ShapeDtypeStruct((MODES, NF), jnp.float32),
        ],
        compiler_params=pltpu.CompilerParams(vmem_limit_bytes=BIG),
        name="solve",
    )(me, scales, sums, start, tiles)


def modes_kernel(after, me_ref, mix_ref, spectra_ref, *refs):
    outs = refs[after:]
    devices = mix_ref.shape[0]
    part = devices // GROUPS
    freqs = outs[0].shape[0]
    per = freqs * MODES * 2
    side = me_ref[0] // part
    for h in range(GROUPS):
        mix = mix_ref[h * part : (h + 1) * part].reshape(part * per, mix_ref.shape[2])
        wide = jnp.dot(mix, spectra_ref[jnp.bitwise_xor(side, h)], preferred_element_type=jnp.float32)
        for near in range(part):
            out = outs[h * part + near]
            for f in range(freqs):
                for k in range(MODES):
                    place = near * per + 2 * (f * MODES + k)
                    out[f, k] = wide[place : place + 2].astype(out.dtype)


def modes_of(me, mix, spectra, after, devices, tile):
    freqs = NF // devices
    groups, rows, size = spectra.shape
    return pl.pallas_call(
        functools.partial(modes_kernel, len(after)),
        grid_spec=pltpu.PrefetchScalarGridSpec(
            num_scalar_prefetch=1,
            grid=(size // tile,),
            in_specs=[
                pl.BlockSpec(mix.shape, lambda g, m: (0, 0, 0)),
                pl.BlockSpec((groups, rows, tile), lambda g, m: (0, 0, g)),
            ]
            + [pl.BlockSpec(memory_space=pl.ANY)] * len(after),
            out_specs=[pl.BlockSpec((freqs, MODES, 2, tile), lambda g, m: (0, 0, 0, g))] * devices,
        ),
        out_shape=[jax.ShapeDtypeStruct((freqs, MODES, 2, size), jnp.bfloat16)] * devices,
        compiler_params=pltpu.CompilerParams(vmem_limit_bytes=BIG),
        name="modes",
    )(me, mix, spectra, *after)


def place_kernel(count, comp, start, size, sub, me_ref, *refs):
    pieces, out_ref, sems = refs[:count], refs[-2], refs[-1]
    me = me_ref[0]
    copies = []
    for place in range(count):
        there = pl.multiple_of(jnp.bitwise_xor(me, place) * sub + start, 128)
        copies.append(
            pltpu.make_async_copy(pieces[place], out_ref.at[:, :, comp, :, pl.ds(there, size)], sems.at[place])
        )
    for copy in copies:
        copy.start()
    for copy in copies:
        copy.wait()


def place(me, pieces, out, comp, start, size, sub, shape):
    count = len(pieces)
    more = [] if out is None else [out]
    return pl.pallas_call(
        functools.partial(place_kernel, count, comp, start, size, sub),
        in_specs=[pl.BlockSpec(memory_space=pltpu.SMEM)]
        + [pl.BlockSpec(memory_space=pltpu.VMEM)] * count
        + [pl.BlockSpec(memory_space=pl.ANY)] * len(more),
        out_specs=pl.BlockSpec(memory_space=pl.ANY),
        out_shape=jax.ShapeDtypeStruct(shape, jnp.bfloat16),
        input_output_aliases={count + 1: 0} if more else {},
        scratch_shapes=[pltpu.SemaphoreType.DMA((count,))],
        compiler_params=pltpu.CompilerParams(vmem_limit_bytes=SMALL),
        name="place",
    )(me, *pieces, *more)


def exchange(pieces, devices):
    landed = [None] * (devices - 1)
    across = list(range(devices // 2, devices))
    inside = list(range(1, devices // 2)) + [0]
    for step in [s for pair in zip(across, inside) for s in pair]:
        if step:
            landed[step - 1] = lax.ppermute(pieces[step - 1], "tm", [(d, d ^ step) for d in range(devices)])
    return landed


def sum_over(value, axis):
    count = lax.axis_size(axis)
    step = 1
    while step < count:
        value = value + lax.ppermute(value, axis, [(d, d ^ step) for d in range(count)])
        step *= 2
    return value


def per_device(snapshots, cell_weights, freq_order):
    devices = lax.axis_size("tm")
    spaces = lax.axis_size("space")
    index = lax.axis_index("tm")
    me = index.astype(jnp.int32).reshape(1)
    half, comps, cells = snapshots.shape
    freqs = NF // devices
    blocks = devices - 1
    padded = -(-blocks // 8) * 8
    rows = blocks * 2 * PER_GROUP
    sub = cells // devices
    unit = sub // QUARTERS
    window = hann_window()
    energy_sum = jnp.sum(window * window)
    scales = jnp.stack([1.0 / (energy_sum * (comps * cells * spaces)), 1.0 / jnp.sqrt(energy_sum)])

    own = jnp.transpose(snapshots, (1, 0, 2))
    weights = cell_weights.reshape(1, cells)
    band = band_table(freq_order, index.astype(jnp.int32), devices)
    line = jnp.arange(rows, dtype=jnp.int32)
    target = line // PER_GROUP % 2 * padded + line // (2 * PER_GROUP)
    fold = (target[None, :] == jnp.arange(2 * padded, dtype=jnp.int32)[:, None]).astype(jnp.float32)
    freq_line = jnp.arange(NF, dtype=jnp.int32)
    tiles = jnp.stack(
        [freq_line[:, None] == g * PER_GROUP + line[None, :] % PER_GROUP for g in range(GROUPS)]
    ).astype(jnp.bfloat16)
    count_a = jnp.arange(padded, dtype=jnp.float32) + 1.0
    count_k = jnp.arange(MODES, dtype=jnp.float32) + 1.0
    start_table = jnp.cos(shift_rate * count_a[None, :] * count_k[:, None])
    start_table = jnp.where(jnp.arange(padded)[None, :] < blocks, start_table, 0.0)
    start_table = jnp.broadcast_to(start_table[:, :, None], (MODES, padded, NF))

    sums = jnp.zeros((GROUPS, 2 * padded, rows), jnp.float32)
    spectra = []
    history = []
    for comp, first, length in CHUNKS_IN:
        start, size = first * unit, length * unit
        pieces = pick(me, own, history[-2:-1], devices, comp, start, size, sub)
        landed = exchange(pieces, devices)
        made, sums = gather(me, band, fold, weights, own, landed, sums, comp, start, size, sub, unit)
        spectra.append(made)
        history.append(sums)
    sums = sum_over(sum_over(sums, "space"), "tm")
    mix, energies = solve(me, scales, sums, start_table, tiles, devices)
    placed = [None]
    shape = (freqs, MODES, comps, 2, cells)
    for chunk in CHUNKS_OUT:
        comp, first, length = CHUNKS_IN[chunk]
        after = [] if len(placed) < 3 else placed[-2:-1]
        made = modes_of(me, mix, spectra[chunk], after, devices, unit)
        landed = [made[0]] + exchange(made[1:], devices)
        placed.append(place(me, landed, placed[-1], comp, first * unit, length * unit, sub, shape))
    mine = lax.dynamic_slice_in_dim(energies, index * freqs, freqs, 1)
    return (jnp.transpose(mine), jnp.transpose(placed[-1], (0, 1, 3, 2, 4)))


def solution(mesh):
    return jax.shard_map(
        per_device,
        mesh=mesh,
        in_specs=(P("tm", None, "space"), P("space"), P()),
        out_specs=(P("tm", None), P("tm", None, None, None, "space")),
        check_vma=False,
    )
```

```python
import functools
import math

import jax
import jax.numpy as jnp
from jax import lax
from jax.experimental import pallas as pl
from jax.experimental.pallas import tpu as pltpu
from jax.sharding import PartitionSpec as P

NFFT = 64
HALF = NFFT // 2
MODES = 4
SWEEPS = 3
NF = 32
GROUPS = 2
PER_GROUP = NF // GROUPS

CHUNKS_IN = ((0, 0, 4), (1, 0, 4), (2, 0, 4))
CHUNKS_OUT = (0, 1, 2)
QUARTERS = 4
EARLY = 0

shift_rate = 0.61
MIB = 1024 * 1024


def vmem(devices):
    return (16 if devices <= 8 else 60) * MIB


def turns(devices):
    across = list(range(devices // 2, devices))
    inside = list(range(1, devices // 2)) + [0]
    return [0] + [t for pair in zip(across, inside) for t in pair][:-1]


def hann_window():
    sample = jnp.arange(NFFT, dtype=jnp.int32)
    return 0.5 - 0.5 * jnp.cos(2.0 * math.pi * sample.astype(jnp.float32) / NFFT)


def window_basis(freqs):
    sample = jnp.arange(NFFT, dtype=jnp.int32)
    turn_index = (freqs[:, None] * sample[None, :] % NFFT).astype(jnp.float32)
    angle_grid = 2.0 * math.pi * turn_index / NFFT
    window = hann_window()
    return jnp.stack([window * jnp.cos(angle_grid), -window * jnp.sin(angle_grid)], 0).astype(jnp.bfloat16)


def band_table(freq_order, me, devices):
    basis = window_basis(freq_order).reshape(2, GROUPS, PER_GROUP, NFFT)
    basis = jnp.transpose(basis, (1, 0, 2, 3))
    half_of = jnp.bitwise_xor(me, jnp.array(turns(devices), jnp.int32))
    block = jnp.arange(devices - 1, dtype=jnp.int32)
    first = (half_of[None, :] == block[:, None])[None, :, None, None, :, None]
    second = (half_of[None, :] == block[:, None] + 1)[None, :, None, None, :, None]
    low = basis[:, None, :, :, None, :HALF]
    high = basis[:, None, :, :, None, HALF:]
    nothing = jnp.zeros((), jnp.bfloat16)
    band = jnp.where(first, low, jnp.where(second, high, nothing))
    return band.reshape(GROUPS, (devices - 1) * 2 * PER_GROUP, devices * HALF)


def pick_kernel(wanted, comp, start, size, sub, me_ref, own_ref, *refs):
    count = len(wanted)
    outs, sems = refs[-count - 1 : -1], refs[-1]
    me = me_ref[0]
    copies = []
    for place, turn in enumerate(wanted):
        there = pl.multiple_of(jnp.bitwise_xor(me, turn) * sub + start, 128)
        copies.append(
            pltpu.make_async_copy(own_ref.at[comp, :, pl.ds(there, size)], outs[place], sems.at[place])
        )
    for copy in copies:
        copy.start()
    for copy in copies:
        copy.wait()


def pick(me, own, after, devices, wanted, comp, start, size, sub):
    count = len(wanted)
    return pl.pallas_call(
        functools.partial(pick_kernel, wanted, comp, start, size, sub),
        in_specs=[pl.BlockSpec(memory_space=pltpu.SMEM)] + [pl.BlockSpec(memory_space=pl.ANY)] * (1 + len(after)),
        out_specs=[pl.BlockSpec(memory_space=pltpu.VMEM)] * count,
        out_shape=[jax.ShapeDtypeStruct((own.shape[1], size), own.dtype)] * count,
        scratch_shapes=[pltpu.SemaphoreType.DMA((count,))],
        compiler_params=pltpu.CompilerParams(vmem_limit_bytes=vmem(devices)),
        name="pick",
    )(me, own, *after)


def gather_kernel(count, me_ref, band_ref, fold_ref, weight_ref, own_ref, *refs):
    landed = refs[:count]
    before_ref, total_ref, sums = refs[count], refs[-2], refs[-1]
    spectra_ref = refs[count + 1] if len(refs) > count + 3 else None
    step = pl.program_id(0)

    @pl.when(step == 0)
    def _():
        sums[...] = jnp.zeros_like(sums)

    data = jnp.concatenate([own_ref[0]] + [ref[...] for ref in landed], 0)
    weight = weight_ref[...]
    for group in range(GROUPS):
        wide = jnp.dot(band_ref[group], data, preferred_element_type=jnp.float32)
        spectra = wide.astype(jnp.bfloat16)
        if spectra_ref is not None:
            spectra_ref[group] = spectra
        weighted = (spectra.astype(jnp.float32) * weight).astype(jnp.bfloat16)
        sums[group] += lax.dot_general(
            weighted, spectra, (((1,), (1,)), ((), ())), preferred_element_type=jnp.float32
        )

    @pl.when(step == pl.num_programs(0) - 1)
    def _():
        rows = sums.shape[1]
        line = lax.broadcasted_iota(jnp.int32, (rows, rows), 0) % PER_GROUP
        column = lax.broadcasted_iota(jnp.int32, (rows, rows), 1) % PER_GROUP
        for group in range(GROUPS):
            kept = jnp.where(line == column, sums[group], 0.0)
            total_ref[group] = before_ref[group] + jnp.dot(
                fold_ref[...], kept, precision=lax.Precision.HIGHEST, preferred_element_type=jnp.float32
            )


def gather(me, band, fold, weights, own, landed, before, keep, comp, start, size, sub, tile):
    count = len(landed)
    devices = count + 1
    half = own.shape[1]
    rows = band.shape[1]
    whole = lambda shape: pl.BlockSpec(shape, lambda g, m: (0,) * len(shape))
    spot = lambda g, m: m[0] * (sub // tile) + start // tile + g
    return pl.pallas_call(
        functools.partial(gather_kernel, count),
        grid_spec=pltpu.PrefetchScalarGridSpec(
            num_scalar_prefetch=1,
            grid=(size // tile,),
            in_specs=[
                whole(band.shape),
                whole(fold.shape),
                pl.BlockSpec((1, tile), lambda g, m: (0, spot(g, m))),
                pl.BlockSpec((1, half, tile), lambda g, m: (comp, 0, spot(g, m))),
            ]
            + [pl.BlockSpec((half, tile), lambda g, m: (0, g))] * count
            + [whole(before.shape)],
            out_specs=[pl.BlockSpec((GROUPS, rows, tile), lambda g, m: (0, 0, g))] * keep + [whole(before.shape)],
            scratch_shapes=[pltpu.VMEM((GROUPS, rows, rows), jnp.float32)],
        ),
        out_shape=[
            jax.ShapeDtypeStruct((GROUPS, rows, size), jnp.bfloat16),
        ]
        * keep
        + [jax.ShapeDtypeStruct(before.shape, jnp.float32)],
        compiler_params=pltpu.CompilerParams(vmem_limit_bytes=vmem(devices)),
        cost_estimate=pl.CostEstimate(
            flops=2 * GROUPS * size * rows * (band.shape[2] + rows), bytes_accessed=2 * size * (2 * rows + 256), transcendentals=0
        ),
        name="gather",
    )(me, band, fold, weights, own, *landed, before)


def solve_kernel(blocks, me_ref, scale_ref, sums_ref, start_ref, tile_ref, mix_ref, energy_ref):
    devices = mix_ref.shape[0]
    freqs = mix_ref.shape[1] // (2 * MODES)
    padded = sums_ref.shape[1] // 2
    gram_scale = scale_ref[0]
    factor = scale_ref[1]

    def lanes(block, part):
        place = (2 * block + part) * PER_GROUP
        return jnp.concatenate([sums_ref[g, :, place : place + PER_GROUP] for g in range(GROUPS)], 1)

    real, imag = [], []
    for block in range(blocks):
        cosine, sine = lanes(block, 0), lanes(block, 1)
        real.append((cosine[:padded] + sine[padded:]) * gram_scale)
        imag.append((sine[:padded] - cosine[padded:]) * gram_scale)

    def apply(vec_re, vec_im):
        out_re = jnp.zeros((padded, NF), jnp.float32)
        out_im = out_re
        for block in range(blocks):
            at_re = vec_re[block : block + 1]
            at_im = vec_im[block : block + 1]
            out_re = out_re + (real[block] * at_re - imag[block] * at_im)
            out_im = out_im + (real[block] * at_im + imag[block] * at_re)
        return out_re, out_im

    def inner(value):
        return jnp.sum(value, axis=0, keepdims=True)

    vectors = [(start_ref[k], jnp.zeros((padded, NF), jnp.float32)) for k in range(MODES)]
    for sweep in range(SWEEPS):
        images = [apply(*vector) for vector in vectors]
        vectors = []
        for col_re, col_im in images:
            for prev_re, prev_im in vectors:
                inner_re = inner(prev_re * col_re + prev_im * col_im)
                inner_im = inner(prev_re * col_im - prev_im * col_re)
                col_re, col_im = (
                    col_re - (inner_re * prev_re - inner_im * prev_im),
                    col_im - (inner_re * prev_im + inner_im * prev_re),
                )
            length = jnp.sqrt(inner(col_re * col_re + col_im * col_im))
            vectors.append((col_re / length, col_im / length))
    for k, (vec_re, vec_im) in enumerate(vectors):
        applied_re, applied_im = apply(vec_re, vec_im)
        energy_ref[k : k + 1] = inner(vec_re * applied_re + vec_im * applied_im)

    straight, turned = [], []
    for vec_re, vec_im in vectors:
        straight += [vec_re * factor, vec_im * factor]
        turned += [-vec_im * factor, vec_re * factor]
    straight = jnp.concatenate(straight, 0).astype(jnp.bfloat16)
    turned = jnp.concatenate(turned, 0).astype(jnp.bfloat16)
    rows = tile_ref.shape[2]
    place = lax.broadcasted_iota(jnp.int32, (2 * MODES, padded, rows), 2)
    mine = place // (2 * PER_GROUP) == lax.broadcasted_iota(jnp.int32, (2 * MODES, padded, rows), 1)
    lane = lax.broadcasted_iota(jnp.int32, (2 * MODES, rows), 1)
    cosine = lane // PER_GROUP % 2 == 0
    me = me_ref[0]

    def spread(value, group):
        wide = jnp.dot(value, tile_ref[group], preferred_element_type=jnp.float32)
        wide = wide.reshape(2 * MODES, padded, rows)
        return jnp.sum(jnp.where(mine, wide, 0.0), axis=1)

    for group in range(GROUPS):
        both = jnp.where(cosine, spread(straight, group), spread(turned, group))
        for near in range(devices // GROUPS):
            device = group * (devices // GROUPS) + near
            pieces = [
                jnp.where(lane % PER_GROUP == near * freqs + f, both, 0.0) for f in range(freqs)
            ]
            mix_ref[jnp.bitwise_xor(me, device)] = jnp.concatenate(pieces, 0).astype(jnp.bfloat16)


def solve(me, scales, sums, start, tiles, devices):
    freqs = NF // devices
    rows = sums.shape[2]
    return pl.pallas_call(
        functools.partial(solve_kernel, devices - 1),
        in_specs=[pl.BlockSpec(memory_space=pltpu.SMEM)] * 2 + [pl.BlockSpec(memory_space=pltpu.VMEM)] * 3,
        out_specs=[pl.BlockSpec(memory_space=pltpu.VMEM)] * 2,
        out_shape=[
            jax.ShapeDtypeStruct((devices, freqs * MODES * 2, rows), jnp.bfloat16),
            jax.ShapeDtypeStruct((MODES, NF), jnp.float32),
        ],
        compiler_params=pltpu.CompilerParams(vmem_limit_bytes=vmem(devices)),
        name="solve",
    )(me, scales, sums, start, tiles)


def fetch_kernel(me_ref, spectra_ref, after_ref, out_ref, sem):
    side = jnp.bitwise_xor(me_ref[0], 1)
    copy = pltpu.make_async_copy(spectra_ref.at[pl.ds(side, 1)], out_ref, sem)
    copy.start()
    copy.wait()


def fetch(side, spectra, after, devices):
    return pl.pallas_call(
        fetch_kernel,
        in_specs=[pl.BlockSpec(memory_space=pltpu.SMEM)] + [pl.BlockSpec(memory_space=pl.ANY)] * 2,
        out_specs=pl.BlockSpec(memory_space=pltpu.VMEM),
        out_shape=jax.ShapeDtypeStruct((1,) + spectra.shape[1:], spectra.dtype),
        scratch_shapes=[pltpu.SemaphoreType.DMA(())],
        compiler_params=pltpu.CompilerParams(vmem_limit_bytes=vmem(devices)),
        name="fetch",
    )(side, spectra, after)


def modes_kernel(after, sides, me_ref, mix_ref, spectra_ref, *refs):
    outs = refs[after:]
    devices = mix_ref.shape[0]
    part = devices // GROUPS
    freqs = outs[0].shape[0]
    per = freqs * MODES * 2
    mine = me_ref[0] // part
    for number, side in enumerate(sides):
        mix = mix_ref[side * part : (side + 1) * part].reshape(part * per, mix_ref.shape[2])
        group = jnp.bitwise_xor(mine, side) if len(sides) > 1 else 0
        wide = jnp.dot(mix, spectra_ref[group], preferred_element_type=jnp.float32)
        for near in range(part):
            split_rows(wide[near * per : (near + 1) * per], outs[number * part + near])


def split_rows(wide, out):
    freqs, modes = out.shape[:2]
    for f in range(freqs):
        for k in range(modes):
            place = 2 * (f * modes + k)
            out[f, k] = wide[place : place + 2].astype(out.dtype)


def modes_of(me, mix, spectra, after, devices, sides, skip, tile):
    freqs = NF // devices
    part = devices // GROUPS
    groups, rows, size = spectra.shape
    count = part * len(sides)
    if groups == 1:
        source = pl.BlockSpec((1, rows, tile), lambda g, m: (0, 0, skip // tile + g))
    elif len(sides) == 1:
        source = pl.BlockSpec(
            (1, rows, tile), lambda g, m: (jnp.bitwise_xor(m[0] // part, sides[0]), 0, skip // tile + g)
        )
    else:
        source = pl.BlockSpec((groups, rows, tile), lambda g, m: (0, 0, skip // tile + g))
    made = pl.pallas_call(
        functools.partial(modes_kernel, len(after), sides),
        grid_spec=pltpu.PrefetchScalarGridSpec(
            num_scalar_prefetch=1,
            grid=((size - skip) // tile,),
            in_specs=[
                pl.BlockSpec(mix.shape, lambda g, m: (0, 0, 0)),
                source,
            ]
            + [pl.BlockSpec(memory_space=pl.ANY)] * len(after),
            out_specs=[pl.BlockSpec((freqs, MODES, 2, tile), lambda g, m: (0, 0, 0, g))] * count,
        ),
        out_shape=[jax.ShapeDtypeStruct((freqs, MODES, 2, size - skip), jnp.bfloat16)] * count,
        compiler_params=pltpu.CompilerParams(vmem_limit_bytes=vmem(devices)),
        name="modes",
    )(me, mix, spectra, *after)
    return {side * part + near: made[n * part + near] for n, side in enumerate(sides) for near in range(part)}


def again_kernel(count, after, me_ref, band_ref, mix_ref, own_ref, *refs):
    landed, outs = refs[:count], refs[count + after :]
    devices = mix_ref.shape[0]
    part = devices // GROUPS
    freqs = outs[0].shape[0]
    per = freqs * MODES * 2
    mine = me_ref[0] // part
    data = jnp.concatenate([own_ref[0]] + [ref[...] for ref in landed], 0)
    for side in (0, 1):
        band = band_ref[jnp.bitwise_xor(mine, side)]
        spectra = jnp.dot(band, data, preferred_element_type=jnp.float32).astype(jnp.bfloat16)
        mix = mix_ref[side * part : (side + 1) * part].reshape(part * per, mix_ref.shape[2])
        wide = jnp.dot(mix, spectra, preferred_element_type=jnp.float32)
        for near in range(part):
            split_rows(wide[near * per : (near + 1) * per], outs[side * part + near])


def modes_again(me, band, mix, own, landed, after, devices, comp, start, size, sub, tile):
    freqs = NF // devices
    count = len(landed)
    half = own.shape[1]
    made = pl.pallas_call(
        functools.partial(again_kernel, count, len(after)),
        grid_spec=pltpu.PrefetchScalarGridSpec(
            num_scalar_prefetch=1,
            grid=(size // tile,),
            in_specs=[
                pl.BlockSpec(band.shape, lambda g, m: (0, 0, 0)),
                pl.BlockSpec(mix.shape, lambda g, m: (0, 0, 0)),
                pl.BlockSpec((1, half, tile), lambda g, m: (comp, 0, m[0] * (sub // tile) + start // tile + g)),
            ]
            + [pl.BlockSpec((half, tile), lambda g, m: (0, g))] * count
            + [pl.BlockSpec(memory_space=pl.ANY)] * len(after),
            out_specs=[pl.BlockSpec((freqs, MODES, 2, tile), lambda g, m: (0, 0, 0, g))] * devices,
        ),
        out_shape=[jax.ShapeDtypeStruct((freqs, MODES, 2, size), jnp.bfloat16)] * devices,
        compiler_params=pltpu.CompilerParams(vmem_limit_bytes=vmem(devices)),
        name="again",
    )(me, band, mix, own, *landed, *after)
    return dict(enumerate(made))


def choose_kernel(me_ref, table_ref, spectra_ref, after_ref, *outs):
    part = len(outs)
    other = jnp.bitwise_xor(me_ref[0] // part, 1)
    for near, out in enumerate(outs):
        out[...] = jnp.dot(table_ref[near], spectra_ref[other], preferred_element_type=jnp.float32).astype(out.dtype)


def choose(me, table, spectra, after, devices, size, tile):
    groups, rows, _ = spectra.shape
    part = devices // GROUPS
    return pl.pallas_call(
        choose_kernel,
        grid_spec=pltpu.PrefetchScalarGridSpec(
            num_scalar_prefetch=1,
            grid=(size // tile,),
            in_specs=[
                pl.BlockSpec(table.shape, lambda g, m: (0, 0, 0)),
                pl.BlockSpec((groups, rows, tile), lambda g, m: (0, 0, g)),
                pl.BlockSpec(memory_space=pl.ANY),
            ],
            out_specs=[pl.BlockSpec((table.shape[1], tile), lambda g, m: (0, g))] * part,
        ),
        out_shape=[jax.ShapeDtypeStruct((table.shape[1], size), jnp.bfloat16)] * part,
        compiler_params=pltpu.CompilerParams(vmem_limit_bytes=vmem(devices)),
        name="choose",
    )(me, table, spectra, after)


def finish_kernel(count, mix_ref, table_ref, *refs):
    mix = lax.dot_general(
        mix_ref[0], table_ref[...], (((1,), (1,)), ((), ())), preferred_element_type=jnp.float32
    ).astype(jnp.bfloat16)
    for landed, out in zip(refs[:count], refs[count:]):
        split_rows(jnp.dot(mix, landed[...], preferred_element_type=jnp.float32), out)


def finish(mix, table, landed, devices, freqs, tile):
    count = len(landed)
    rows, size = landed[0].shape
    return pl.pallas_call(
        functools.partial(finish_kernel, count),
        grid=(size // tile,),
        in_specs=[
            pl.BlockSpec((1,) + mix.shape[1:], lambda g: (0, 0, 0)),
            pl.BlockSpec(table.shape, lambda g: (0, 0)),
        ]
        + [pl.BlockSpec((rows, tile), lambda g: (0, g))] * count,
        out_specs=[pl.BlockSpec((freqs, MODES, 2, tile), lambda g: (0, 0, 0, g))] * count,
        out_shape=[jax.ShapeDtypeStruct((freqs, MODES, 2, size), jnp.bfloat16)] * count,
        compiler_params=pltpu.CompilerParams(vmem_limit_bytes=vmem(devices)),
        name="finish",
    )(mix, table, *landed)


def place_kernel(spots, comp, sub, me_ref, *refs):
    count = len(spots)
    pieces, out_ref, sems = refs[:count], refs[-2], refs[-1]
    me = me_ref[0]
    copies = []
    for n, (turn, start) in enumerate(spots):
        there = pl.multiple_of(jnp.bitwise_xor(me, turn) * sub + start, 128)
        copies.append(
            pltpu.make_async_copy(
                pieces[n], out_ref.at[:, :, comp, :, pl.ds(there, pieces[n].shape[3])], sems.at[n]
            )
        )
    for copy in copies:
        copy.start()
    for copy in copies:
        copy.wait()


def place(me, pieces, out, devices, comp, sub, shape):
    arrays = [piece[0] for piece in pieces]
    count = len(pieces)
    more = [] if out is None else [out]
    return pl.pallas_call(
        functools.partial(place_kernel, [piece[1:] for piece in pieces], comp, sub),
        in_specs=[pl.BlockSpec(memory_space=pltpu.SMEM)]
        + [pl.BlockSpec(memory_space=pltpu.VMEM)] * count
        + [pl.BlockSpec(memory_space=pl.ANY)] * len(more),
        out_specs=pl.BlockSpec(memory_space=pl.ANY),
        out_shape=jax.ShapeDtypeStruct(shape, jnp.bfloat16),
        input_output_aliases={count + 1: 0} if more else {},
        scratch_shapes=[pltpu.SemaphoreType.DMA((count,))],
        compiler_params=pltpu.CompilerParams(vmem_limit_bytes=vmem(devices)),
        name="place",
    )(me, *arrays, *more)


def send(value, turn, devices):
    return lax.ppermute(value, "tm", [(d, d ^ turn) for d in range(devices)])


def exchange(pieces, devices):
    return [send(piece, turn, devices) for piece, turn in zip(pieces, turns(devices)[1:])]


def sum_over(value, axis):
    count = lax.axis_size(axis)
    step = 1
    while step < count:
        value = value + lax.ppermute(value, axis, [(d, d ^ step) for d in range(count)])
        step *= 2
    return value


def per_device(snapshots, cell_weights, freq_order):
    devices = lax.axis_size("tm")
    spaces = lax.axis_size("space")
    index = lax.axis_index("tm")
    me = index.astype(jnp.int32).reshape(1)
    half, comps, cells = snapshots.shape
    freqs = NF // devices
    blocks = devices - 1
    padded = -(-blocks // 8) * 8
    rows = blocks * 2 * PER_GROUP
    sub = cells // devices
    unit = sub // QUARTERS
    window = hann_window()
    energy_sum = jnp.sum(window * window)
    scales = jnp.stack([1.0 / (energy_sum * (comps * cells * spaces)), 1.0 / jnp.sqrt(energy_sum)])

    own = jnp.transpose(snapshots, (1, 0, 2))
    weights = cell_weights.reshape(1, cells)
    band = band_table(freq_order, index.astype(jnp.int32), devices)
    line = jnp.arange(rows, dtype=jnp.int32)
    target = line // PER_GROUP % 2 * padded + line // (2 * PER_GROUP)
    fold = (target[None, :] == jnp.arange(2 * padded, dtype=jnp.int32)[:, None]).astype(jnp.float32)
    freq_line = jnp.arange(NF, dtype=jnp.int32)
    tiles = jnp.stack(
        [freq_line[:, None] == g * PER_GROUP + line[None, :] % PER_GROUP for g in range(GROUPS)]
    ).astype(jnp.bfloat16)
    count_a = jnp.arange(padded, dtype=jnp.float32) + 1.0
    count_k = jnp.arange(MODES, dtype=jnp.float32) + 1.0
    start_table = jnp.cos(shift_rate * count_a[None, :] * count_k[:, None])
    start_table = jnp.where(jnp.arange(padded)[None, :] < blocks, start_table, 0.0)
    start_table = jnp.broadcast_to(start_table[:, :, None], (MODES, padded, NF))

    sums = jnp.zeros((GROUPS, 2 * padded, rows), jnp.float32)
    spectra = []
    history = []
    for comp, first, length in CHUNKS_IN:
        start, size = first * unit, length * unit
        order = turns(devices)[1:]
        cut = 0 if history else 1
        pieces = []
        for wanted in (order[:cut], order[cut:]):
            if wanted:
                pieces += pick(me, own, history[-2:-1], devices, wanted, comp, start, size, sub)
        landed = exchange(pieces, devices)
        keep = len(history) < len(CHUNKS_IN) - 1
        *made, sums = gather(me, band, fold, weights, own, landed, sums, keep, comp, start, size, sub, unit if keep else 4 * unit)
        spectra += made
        history.append(sums)
    part = devices // GROUPS
    early = EARLY * unit // 2
    lines = jnp.arange(blocks * 2 * freqs, dtype=jnp.int32)
    near = jnp.bitwise_xor(index.astype(jnp.int32), jnp.arange(part, dtype=jnp.int32)) % part
    same_part = (lines // freqs)[:, None] == (line // PER_GROUP)[None, :]
    wanted = (near[:, None] * freqs + lines % freqs)[:, :, None] == (line % PER_GROUP)[None, None, :]
    table = (same_part[None] & wanted).astype(jnp.bfloat16)
    crossed = []
    if early:
        chosen = choose(me, table, spectra[0], history[-2], devices, early, unit // 2)
        crossed = [send(value, part + n, devices) for n, value in enumerate(chosen)]

    sums = sum_over(sums, "space")
    ready = fetch(me // part, spectra[0], sums, devices)
    sums = sum_over(sums, "tm")
    mix, energies = solve(me, scales, sums, start_table, tiles, devices)
    placed = [None]
    shape = (freqs, MODES, comps, 2, cells)
    for chunk in CHUNKS_OUT:
        comp, first, length = CHUNKS_IN[chunk]
        after = [] if len(placed) < 3 else placed[-2:-1]
        pieces = []
        if chunk == 0:
            made = modes_of(me, mix, ready, after, devices, (1,), early, 4 * unit)
            made.update(modes_of(me, mix, spectra[0], after, devices, (0,), 0, unit))
        elif chunk == len(CHUNKS_IN) - 1:
            made = modes_again(
                me, band, mix, own, landed, after, devices, comp, first * unit, length * unit, sub, unit
            )
        else:
            made = modes_of(me, mix, spectra[chunk], after, devices, (0, 1), 0, unit)
        for turn in turns(devices):
            skip = early if chunk == 0 and turn >= part else 0
            value = send(made[turn], turn, devices) if turn else made[turn]
            pieces.append((value, turn, first * unit + skip))
        if chunk == 0 and early:
            late = finish(mix, table[0], crossed, devices, freqs, unit // 2)
            pieces += [(value, part + n, first * unit) for n, value in enumerate(late)]
        soon = pieces[:5] if chunk == CHUNKS_OUT[-1] else []
        done = place(me, soon, placed[-1], devices, comp, sub, shape) if soon else placed[-1]
        placed.append(place(me, pieces[len(soon) :], done, devices, comp, sub, shape))
    mine = lax.dynamic_slice_in_dim(energies, index * freqs, freqs, 1)
    return (jnp.transpose(mine), jnp.transpose(placed[-1], (0, 1, 3, 2, 4)))


def solution(mesh):
    return jax.shard_map(
        per_device,
        mesh=mesh,
        in_specs=(P("tm", None, "space"), P("space"), P()),
        out_specs=(P("tm", None), P("tm", None, None, None, "space")),
        check_vma=False,
    )
```

```python
import functools
import math

import jax
import jax.numpy as jnp
from jax import lax
from jax.experimental import pallas as pl
from jax.experimental.pallas import tpu as pltpu
from jax.sharding import PartitionSpec as P

NFFT = 64
HALF = NFFT // 2
MODES = 4
SWEEPS = 3
NF = 32
GROUPS = 2
PER_GROUP = NF // GROUPS

CHUNKS_IN = ((0, 0, 4), (1, 0, 4), (2, 0, 4))
CHUNKS_OUT = (0, 1, 2)
QUARTERS = 4

shift_rate = 0.61
MIB = 1024 * 1024


def vmem(devices):
    return (16 if devices <= 8 else 60) * MIB


def turns(devices):
    across = list(range(devices // 2, devices))
    inside = list(range(1, devices // 2)) + [0]
    return [0] + [t for pair in zip(across, inside) for t in pair][:-1]


def hann_window():
    sample = jnp.arange(NFFT, dtype=jnp.int32)
    return 0.5 - 0.5 * jnp.cos(2.0 * math.pi * sample.astype(jnp.float32) / NFFT)


def window_basis(freqs):
    sample = jnp.arange(NFFT, dtype=jnp.int32)
    turn_index = (freqs[:, None] * sample[None, :] % NFFT).astype(jnp.float32)
    angle_grid = 2.0 * math.pi * turn_index / NFFT
    window = hann_window()
    return jnp.stack([window * jnp.cos(angle_grid), -window * jnp.sin(angle_grid)], 0).astype(jnp.bfloat16)


def band_table(freq_order, me, devices):
    basis = window_basis(freq_order).reshape(2, GROUPS, PER_GROUP, NFFT)
    basis = jnp.transpose(basis, (1, 0, 2, 3))
    half_of = jnp.bitwise_xor(me, jnp.array(turns(devices), jnp.int32))
    block = jnp.arange(devices - 1, dtype=jnp.int32)
    first = (half_of[None, :] == block[:, None])[None, :, None, None, :, None]
    second = (half_of[None, :] == block[:, None] + 1)[None, :, None, None, :, None]
    low = basis[:, None, :, :, None, :HALF]
    high = basis[:, None, :, :, None, HALF:]
    nothing = jnp.zeros((), jnp.bfloat16)
    band = jnp.where(first, low, jnp.where(second, high, nothing))
    return band.reshape(GROUPS, (devices - 1) * 2 * PER_GROUP, devices * HALF)


def pick_kernel(wanted, comp, start, size, sub, me_ref, own_ref, *refs):
    count = len(wanted)
    outs, sems = refs[-count - 1 : -1], refs[-1]
    me = me_ref[0]
    copies = []
    for place, turn in enumerate(wanted):
        there = pl.multiple_of(jnp.bitwise_xor(me, turn) * sub + start, 128)
        copies.append(
            pltpu.make_async_copy(own_ref.at[comp, :, pl.ds(there, size)], outs[place], sems.at[place])
        )
    for copy in copies:
        copy.start()
    for copy in copies:
        copy.wait()


def pick(me, own, after, devices, wanted, comp, start, size, sub):
    count = len(wanted)
    return pl.pallas_call(
        functools.partial(pick_kernel, wanted, comp, start, size, sub),
        in_specs=[pl.BlockSpec(memory_space=pltpu.SMEM)] + [pl.BlockSpec(memory_space=pl.ANY)] * (1 + len(after)),
        out_specs=[pl.BlockSpec(memory_space=pltpu.VMEM)] * count,
        out_shape=[jax.ShapeDtypeStruct((own.shape[1], size), own.dtype)] * count,
        scratch_shapes=[pltpu.SemaphoreType.DMA((count,))],
        compiler_params=pltpu.CompilerParams(vmem_limit_bytes=60 * MIB if len(wanted) < devices - 1 else vmem(devices)),
        name="pick",
    )(me, own, *after)


def gather_kernel(count, me_ref, band_ref, fold_ref, weight_ref, own_ref, *refs):
    landed = refs[:count]
    before_ref, total_ref, sums = refs[count], refs[-2], refs[-1]
    spectra_ref = refs[count + 1] if len(refs) > count + 3 else None
    step = pl.program_id(0)

    @pl.when(step == 0)
    def _():
        sums[...] = jnp.zeros_like(sums)

    data = jnp.concatenate([own_ref[0]] + [ref[...] for ref in landed], 0)
    weight = weight_ref[...]
    for group in range(GROUPS):
        wide = jnp.dot(band_ref[group], data, preferred_element_type=jnp.float32)
        spectra = wide.astype(jnp.bfloat16)
        if spectra_ref is not None:
            spectra_ref[group] = spectra
        weighted = (spectra.astype(jnp.float32) * weight).astype(jnp.bfloat16)
        sums[group] += lax.dot_general(
            weighted, spectra, (((1,), (1,)), ((), ())), preferred_element_type=jnp.float32
        )

    @pl.when(step == pl.num_programs(0) - 1)
    def _():
        rows = sums.shape[1]
        line = lax.broadcasted_iota(jnp.int32, (rows, rows), 0) % PER_GROUP
        column = lax.broadcasted_iota(jnp.int32, (rows, rows), 1) % PER_GROUP
        for group in range(GROUPS):
            kept = jnp.where(line == column, sums[group], 0.0)
            total_ref[group] = before_ref[group] + jnp.dot(
                fold_ref[...], kept, precision=lax.Precision.HIGHEST, preferred_element_type=jnp.float32
            )


def gather(me, band, fold, weights, own, landed, before, keep, comp, start, size, sub, tile):
    count = len(landed)
    devices = count + 1
    half = own.shape[1]
    rows = band.shape[1]
    whole = lambda shape: pl.BlockSpec(shape, lambda g, m: (0,) * len(shape))
    spot = lambda g, m: m[0] * (sub // tile) + start // tile + g
    return pl.pallas_call(
        functools.partial(gather_kernel, count),
        grid_spec=pltpu.PrefetchScalarGridSpec(
            num_scalar_prefetch=1,
            grid=(size // tile,),
            in_specs=[
                whole(band.shape),
                whole(fold.shape),
                pl.BlockSpec((1, tile), lambda g, m: (0, spot(g, m))),
                pl.BlockSpec((1, half, tile), lambda g, m: (comp, 0, spot(g, m))),
            ]
            + [pl.BlockSpec((half, tile), lambda g, m: (0, g))] * count
            + [whole(before.shape)],
            out_specs=[pl.BlockSpec((GROUPS, rows, tile), lambda g, m: (0, 0, g))] * keep + [whole(before.shape)],
            scratch_shapes=[pltpu.VMEM((GROUPS, rows, rows), jnp.float32)],
        ),
        out_shape=[
            jax.ShapeDtypeStruct((GROUPS, rows, size), jnp.bfloat16),
        ]
        * keep
        + [jax.ShapeDtypeStruct(before.shape, jnp.float32)],
        compiler_params=pltpu.CompilerParams(vmem_limit_bytes=vmem(devices)),
        cost_estimate=pl.CostEstimate(
            flops=2 * GROUPS * size * rows * (band.shape[2] + rows), bytes_accessed=2 * size * (2 * rows + 256), transcendentals=0
        ),
        name="gather",
    )(me, band, fold, weights, own, *landed, before)


def solve_kernel(blocks, me_ref, scale_ref, sums_ref, start_ref, tile_ref, mix_ref, energy_ref):
    devices = mix_ref.shape[0]
    freqs = mix_ref.shape[1] // (2 * MODES)
    padded = sums_ref.shape[1] // 2
    gram_scale = scale_ref[0]
    factor = scale_ref[1]

    def lanes(block, part):
        place = (2 * block + part) * PER_GROUP
        return jnp.concatenate([sums_ref[g, :, place : place + PER_GROUP] for g in range(GROUPS)], 1)

    real, imag = [], []
    for block in range(blocks):
        cosine, sine = lanes(block, 0), lanes(block, 1)
        real.append((cosine[:padded] + sine[padded:]) * gram_scale)
        imag.append((sine[:padded] - cosine[padded:]) * gram_scale)

    def apply(vec_re, vec_im):
        out_re = jnp.zeros((padded, NF), jnp.float32)
        out_im = out_re
        for block in range(blocks):
            at_re = vec_re[block : block + 1]
            at_im = vec_im[block : block + 1]
            out_re = out_re + (real[block] * at_re - imag[block] * at_im)
            out_im = out_im + (real[block] * at_im + imag[block] * at_re)
        return out_re, out_im

    def inner(value):
        return jnp.sum(value, axis=0, keepdims=True)

    vectors = [(start_ref[k], jnp.zeros((padded, NF), jnp.float32)) for k in range(MODES)]
    for sweep in range(SWEEPS):
        images = [apply(*vector) for vector in vectors]
        vectors = []
        for col_re, col_im in images:
            for prev_re, prev_im in vectors:
                inner_re = inner(prev_re * col_re + prev_im * col_im)
                inner_im = inner(prev_re * col_im - prev_im * col_re)
                col_re, col_im = (
                    col_re - (inner_re * prev_re - inner_im * prev_im),
                    col_im - (inner_re * prev_im + inner_im * prev_re),
                )
            length = jnp.sqrt(inner(col_re * col_re + col_im * col_im))
            vectors.append((col_re / length, col_im / length))
    for k, (vec_re, vec_im) in enumerate(vectors):
        applied_re, applied_im = apply(vec_re, vec_im)
        energy_ref[k : k + 1] = inner(vec_re * applied_re + vec_im * applied_im)

    straight, turned = [], []
    for vec_re, vec_im in vectors:
        straight += [vec_re * factor, vec_im * factor]
        turned += [-vec_im * factor, vec_re * factor]
    straight = jnp.concatenate(straight, 0).astype(jnp.bfloat16)
    turned = jnp.concatenate(turned, 0).astype(jnp.bfloat16)
    rows = tile_ref.shape[2]
    place = lax.broadcasted_iota(jnp.int32, (2 * MODES, padded, rows), 2)
    mine = place // (2 * PER_GROUP) == lax.broadcasted_iota(jnp.int32, (2 * MODES, padded, rows), 1)
    lane = lax.broadcasted_iota(jnp.int32, (2 * MODES, rows), 1)
    cosine = lane // PER_GROUP % 2 == 0
    me = me_ref[0]

    def spread(value, group):
        wide = jnp.dot(value, tile_ref[group], preferred_element_type=jnp.float32)
        wide = wide.reshape(2 * MODES, padded, rows)
        return jnp.sum(jnp.where(mine, wide, 0.0), axis=1)

    for group in range(GROUPS):
        both = jnp.where(cosine, spread(straight, group), spread(turned, group))
        for near in range(devices // GROUPS):
            device = group * (devices // GROUPS) + near
            pieces = [
                jnp.where(lane % PER_GROUP == near * freqs + f, both, 0.0) for f in range(freqs)
            ]
            mix_ref[jnp.bitwise_xor(me, device)] = jnp.concatenate(pieces, 0).astype(jnp.bfloat16)


def solve(me, scales, sums, start, tiles, devices):
    freqs = NF // devices
    rows = sums.shape[2]
    return pl.pallas_call(
        functools.partial(solve_kernel, devices - 1),
        in_specs=[pl.BlockSpec(memory_space=pltpu.SMEM)] * 2 + [pl.BlockSpec(memory_space=pltpu.VMEM)] * 3,
        out_specs=[pl.BlockSpec(memory_space=pltpu.VMEM)] * 2,
        out_shape=[
            jax.ShapeDtypeStruct((devices, freqs * MODES * 2, rows), jnp.bfloat16),
            jax.ShapeDtypeStruct((MODES, NF), jnp.float32),
        ],
        compiler_params=pltpu.CompilerParams(vmem_limit_bytes=vmem(devices)),
        name="solve",
    )(me, scales, sums, start, tiles)


def fetch_kernel(spectra_ref, after_ref, out_ref, sem):
    copy = pltpu.make_async_copy(spectra_ref, out_ref, sem)
    copy.start()
    copy.wait()


def fetch(spectra, after, devices):
    return pl.pallas_call(
        fetch_kernel,
        in_specs=[pl.BlockSpec(memory_space=pl.ANY)] * 2,
        out_specs=pl.BlockSpec(memory_space=pltpu.VMEM),
        out_shape=jax.ShapeDtypeStruct(spectra.shape, spectra.dtype),
        scratch_shapes=[pltpu.SemaphoreType.DMA(())],
        compiler_params=pltpu.CompilerParams(vmem_limit_bytes=vmem(devices)),
        name="fetch",
    )(spectra, after)


def modes_kernel(after, sides, me_ref, mix_ref, spectra_ref, *refs):
    outs = refs[after:]
    devices = mix_ref.shape[0]
    part = devices // GROUPS
    freqs = outs[0].shape[0]
    per = freqs * MODES * 2
    mine = me_ref[0] // part
    for number, side in enumerate(sides):
        mix = mix_ref[side * part : (side + 1) * part].reshape(part * per, mix_ref.shape[2])
        group = jnp.bitwise_xor(mine, side) if len(sides) > 1 else 0
        wide = jnp.dot(mix, spectra_ref[group], preferred_element_type=jnp.float32)
        for near in range(part):
            split_rows(wide[near * per : (near + 1) * per], outs[number * part + near])


def split_rows(wide, out):
    freqs, modes = out.shape[:2]
    for f in range(freqs):
        for k in range(modes):
            place = 2 * (f * modes + k)
            out[f, k] = wide[place : place + 2].astype(out.dtype)


def modes_of(me, mix, spectra, after, devices, sides, tile):
    freqs = NF // devices
    part = devices // GROUPS
    groups, rows, size = spectra.shape
    count = part * len(sides)
    if len(sides) == 1:
        source = pl.BlockSpec(
            (1, rows, tile), lambda g, m: (jnp.bitwise_xor(m[0] // part, sides[0]), 0, g)
        )
    else:
        source = pl.BlockSpec((groups, rows, tile), lambda g, m: (0, 0, g))
    made = pl.pallas_call(
        functools.partial(modes_kernel, len(after), sides),
        grid_spec=pltpu.PrefetchScalarGridSpec(
            num_scalar_prefetch=1,
            grid=(size // tile,),
            in_specs=[
                pl.BlockSpec(mix.shape, lambda g, m: (0, 0, 0)),
                source,
            ]
            + [pl.BlockSpec(memory_space=pl.ANY)] * len(after),
            out_specs=[pl.BlockSpec((freqs, MODES, 2, tile), lambda g, m: (0, 0, 0, g))] * count,
        ),
        out_shape=[jax.ShapeDtypeStruct((freqs, MODES, 2, size), jnp.bfloat16)] * count,
        compiler_params=pltpu.CompilerParams(vmem_limit_bytes=vmem(devices)),
        name="modes",
    )(me, mix, spectra, *after)
    return {side * part + near: made[n * part + near] for n, side in enumerate(sides) for near in range(part)}


def again_kernel(count, after, me_ref, band_ref, mix_ref, own_ref, *refs):
    landed, outs = refs[:count], refs[count + after :]
    devices = mix_ref.shape[0]
    part = devices // GROUPS
    freqs = outs[0].shape[0]
    per = freqs * MODES * 2
    mine = me_ref[0] // part
    data = jnp.concatenate([own_ref[0]] + [ref[...] for ref in landed], 0)
    for side in (0, 1):
        band = band_ref[jnp.bitwise_xor(mine, side)]
        spectra = jnp.dot(band, data, preferred_element_type=jnp.float32).astype(jnp.bfloat16)
        mix = mix_ref[side * part : (side + 1) * part].reshape(part * per, mix_ref.shape[2])
        wide = jnp.dot(mix, spectra, preferred_element_type=jnp.float32)
        for near in range(part):
            split_rows(wide[near * per : (near + 1) * per], outs[side * part + near])


def modes_again(me, band, mix, own, landed, after, devices, comp, start, size, sub, tile):
    freqs = NF // devices
    count = len(landed)
    half = own.shape[1]
    made = pl.pallas_call(
        functools.partial(again_kernel, count, len(after)),
        grid_spec=pltpu.PrefetchScalarGridSpec(
            num_scalar_prefetch=1,
            grid=(size // tile,),
            in_specs=[
                pl.BlockSpec(band.shape, lambda g, m: (0, 0, 0)),
                pl.BlockSpec(mix.shape, lambda g, m: (0, 0, 0)),
                pl.BlockSpec((1, half, tile), lambda g, m: (comp, 0, m[0] * (sub // tile) + start // tile + g)),
            ]
            + [pl.BlockSpec((half, tile), lambda g, m: (0, g))] * count
            + [pl.BlockSpec(memory_space=pl.ANY)] * len(after),
            out_specs=[pl.BlockSpec((freqs, MODES, 2, tile), lambda g, m: (0, 0, 0, g))] * devices,
        ),
        out_shape=[jax.ShapeDtypeStruct((freqs, MODES, 2, size), jnp.bfloat16)] * devices,
        compiler_params=pltpu.CompilerParams(vmem_limit_bytes=vmem(devices)),
        name="again",
    )(me, band, mix, own, *landed, *after)
    return dict(enumerate(made))


def place_kernel(spots, comp, sub, me_ref, *refs):
    count = len(spots)
    pieces, out_ref, sems = refs[:count], refs[-2], refs[-1]
    me = me_ref[0]
    copies = []
    for n, (turn, start) in enumerate(spots):
        there = pl.multiple_of(jnp.bitwise_xor(me, turn) * sub + start, 128)
        copies.append(
            pltpu.make_async_copy(
                pieces[n], out_ref.at[:, :, comp, :, pl.ds(there, pieces[n].shape[3])], sems.at[n]
            )
        )
    for copy in copies:
        copy.start()
    for copy in copies:
        copy.wait()


def place(me, pieces, out, devices, comp, sub, shape):
    arrays = [piece[0] for piece in pieces]
    count = len(pieces)
    more = [] if out is None else [out]
    return pl.pallas_call(
        functools.partial(place_kernel, [piece[1:] for piece in pieces], comp, sub),
        in_specs=[pl.BlockSpec(memory_space=pltpu.SMEM)]
        + [pl.BlockSpec(memory_space=pltpu.VMEM)] * count
        + [pl.BlockSpec(memory_space=pl.ANY)] * len(more),
        out_specs=pl.BlockSpec(memory_space=pl.ANY),
        out_shape=jax.ShapeDtypeStruct(shape, jnp.bfloat16),
        input_output_aliases={count + 1: 0} if more else {},
        scratch_shapes=[pltpu.SemaphoreType.DMA((count,))],
        compiler_params=pltpu.CompilerParams(vmem_limit_bytes=vmem(devices)),
        name="place",
    )(me, *arrays, *more)


def send(value, turn, devices):
    return lax.ppermute(value, "tm", [(d, d ^ turn) for d in range(devices)])


def exchange(pieces, devices):
    return [send(piece, turn, devices) for piece, turn in zip(pieces, turns(devices)[1:])]


def sum_over(value, axis):
    count = lax.axis_size(axis)
    step = 1
    while step < count:
        value = value + lax.ppermute(value, axis, [(d, d ^ step) for d in range(count)])
        step *= 2
    return value


def per_device(snapshots, cell_weights, freq_order):
    devices = lax.axis_size("tm")
    spaces = lax.axis_size("space")
    index = lax.axis_index("tm")
    me = index.astype(jnp.int32).reshape(1)
    half, comps, cells = snapshots.shape
    freqs = NF // devices
    blocks = devices - 1
    padded = -(-blocks // 8) * 8
    rows = blocks * 2 * PER_GROUP
    sub = cells // devices
    unit = sub // QUARTERS
    window = hann_window()
    energy_sum = jnp.sum(window * window)
    scales = jnp.stack([1.0 / (energy_sum * (comps * cells * spaces)), 1.0 / jnp.sqrt(energy_sum)])

    own = jnp.transpose(snapshots, (1, 0, 2))
    weights = cell_weights.reshape(1, cells)
    band = band_table(freq_order, index.astype(jnp.int32), devices)
    line = jnp.arange(rows, dtype=jnp.int32)
    target = line // PER_GROUP % 2 * padded + line // (2 * PER_GROUP)
    fold = (target[None, :] == jnp.arange(2 * padded, dtype=jnp.int32)[:, None]).astype(jnp.float32)
    freq_line = jnp.arange(NF, dtype=jnp.int32)
    tiles = jnp.stack(
        [freq_line[:, None] == g * PER_GROUP + line[None, :] % PER_GROUP for g in range(GROUPS)]
    ).astype(jnp.bfloat16)
    count_a = jnp.arange(padded, dtype=jnp.float32) + 1.0
    count_k = jnp.arange(MODES, dtype=jnp.float32) + 1.0
    start_table = jnp.cos(shift_rate * count_a[None, :] * count_k[:, None])
    start_table = jnp.where(jnp.arange(padded)[None, :] < blocks, start_table, 0.0)
    start_table = jnp.broadcast_to(start_table[:, :, None], (MODES, padded, NF))

    sums = jnp.zeros((GROUPS, 2 * padded, rows), jnp.float32)
    spectra = []
    history = []
    for comp, first, length in CHUNKS_IN:
        start, size = first * unit, length * unit
        order = turns(devices)[1:]
        cut = 0 if history else 1
        pieces = []
        for wanted in (order[:cut], order[cut:]):
            if wanted:
                pieces += pick(me, own, history[-2:-1], devices, wanted, comp, start, size, sub)
        landed = exchange(pieces, devices)
        keep = len(history) < len(CHUNKS_IN) - 1
        *made, sums = gather(me, band, fold, weights, own, landed, sums, keep, comp, start, size, sub, unit if keep else 4 * unit)
        spectra += made
        history.append(sums)
    sums = sum_over(sums, "space")
    ready = fetch(spectra[0], sums, devices)
    sums = sum_over(sums, "tm")
    mix, energies = solve(me, scales, sums, start_table, tiles, devices)
    placed = [None]
    shape = (freqs, MODES, comps, 2, cells)
    for chunk in CHUNKS_OUT:
        comp, first, length = CHUNKS_IN[chunk]
        after = [] if len(placed) < 3 else placed[-2:-1]
        pieces = []
        if chunk == 0:
            made = modes_of(me, mix, ready, after, devices, (1,), QUARTERS * unit)
            made.update(modes_of(me, mix, ready, after, devices, (0,), unit))
        elif chunk == len(CHUNKS_IN) - 1:
            made = modes_again(
                me, band, mix, own, landed, after, devices, comp, first * unit, length * unit, sub, unit
            )
        else:
            made = modes_of(me, mix, spectra[chunk], after, devices, (0, 1), unit)
        for turn in turns(devices):
            value = send(made[turn], turn, devices) if turn else made[turn]
            pieces.append((value, turn, first * unit))
        soon = pieces[:6] if chunk == CHUNKS_OUT[-1] else []
        done = place(me, soon, placed[-1], devices, comp, sub, shape) if soon else placed[-1]
        placed.append(place(me, pieces[len(soon) :], done, devices, comp, sub, shape))
    mine = lax.dynamic_slice_in_dim(energies, index * freqs, freqs, 1)
    return (jnp.transpose(mine), jnp.transpose(placed[-1], (0, 1, 3, 2, 4)))


def solution(mesh):
    return jax.shard_map(
        per_device,
        mesh=mesh,
        in_specs=(P("tm", None, "space"), P("space"), P()),
        out_specs=(P("tm", None), P("tm", None, None, None, "space")),
        check_vma=False,
    )
```

```python
import functools
import math

import jax
import jax.numpy as jnp
from jax import lax
from jax.experimental import pallas as pl
from jax.experimental.pallas import tpu as pltpu
from jax.sharding import PartitionSpec as P

NFFT = 64
HALF = NFFT // 2
MODES = 4
SWEEPS = 3
NF = 32
GROUPS = 2
PER_GROUP = NF // GROUPS

CHUNKS_IN = ((0, 0, 4), (1, 0, 4), (2, 0, 4))
CHUNKS_OUT = (0, 1, 2)
QUARTERS = 4

shift_rate = 0.61
MIB = 1024 * 1024


def vmem(devices):
    return (16 if devices <= 8 else 60) * MIB


def turns(devices):
    across = list(range(devices // 2, devices))
    inside = list(range(1, devices // 2)) + [0]
    return [0] + [t for pair in zip(across, inside) for t in pair][:-1]


def hann_window():
    sample = jnp.arange(NFFT, dtype=jnp.int32)
    return 0.5 - 0.5 * jnp.cos(2.0 * math.pi * sample.astype(jnp.float32) / NFFT)


def window_basis(freqs):
    sample = jnp.arange(NFFT, dtype=jnp.int32)
    turn_index = (freqs[:, None] * sample[None, :] % NFFT).astype(jnp.float32)
    angle_grid = 2.0 * math.pi * turn_index / NFFT
    window = hann_window()
    return jnp.stack([window * jnp.cos(angle_grid), -window * jnp.sin(angle_grid)], 0).astype(jnp.bfloat16)


def band_table(freq_order, me, devices):
    basis = window_basis(freq_order).reshape(2, GROUPS, PER_GROUP, NFFT)
    basis = jnp.transpose(basis, (1, 0, 2, 3))
    half_of = jnp.bitwise_xor(me, jnp.array(turns(devices), jnp.int32))
    block = jnp.arange(devices - 1, dtype=jnp.int32)
    first = (half_of[None, :] == block[:, None])[None, :, None, None, :, None]
    second = (half_of[None, :] == block[:, None] + 1)[None, :, None, None, :, None]
    low = basis[:, None, :, :, None, :HALF]
    high = basis[:, None, :, :, None, HALF:]
    nothing = jnp.zeros((), jnp.bfloat16)
    band = jnp.where(first, low, jnp.where(second, high, nothing))
    return band.reshape(GROUPS, (devices - 1) * 2 * PER_GROUP, devices * HALF)


def pick_kernel(wanted, comp, start, size, sub, me_ref, own_ref, *refs):
    count = len(wanted)
    outs, sems = refs[-count - 1 : -1], refs[-1]
    me = me_ref[0]
    copies = []
    for place, turn in enumerate(wanted):
        there = pl.multiple_of(jnp.bitwise_xor(me, turn) * sub + start, 128)
        copies.append(
            pltpu.make_async_copy(own_ref.at[comp, :, pl.ds(there, size)], outs[place], sems.at[place])
        )
    for copy in copies:
        copy.start()
    for copy in copies:
        copy.wait()


def pick(me, own, after, devices, wanted, comp, start, size, sub):
    count = len(wanted)
    return pl.pallas_call(
        functools.partial(pick_kernel, wanted, comp, start, size, sub),
        in_specs=[pl.BlockSpec(memory_space=pltpu.SMEM)] + [pl.BlockSpec(memory_space=pl.ANY)] * (1 + len(after)),
        out_specs=[pl.BlockSpec(memory_space=pltpu.VMEM)] * count,
        out_shape=[jax.ShapeDtypeStruct((own.shape[1], size), own.dtype)] * count,
        scratch_shapes=[pltpu.SemaphoreType.DMA((count,))],
        compiler_params=pltpu.CompilerParams(vmem_limit_bytes=60 * MIB if len(wanted) < devices - 1 else vmem(devices)),
        name="pick",
    )(me, own, *after)


def gather_kernel(count, me_ref, band_ref, fold_ref, weight_ref, own_ref, *refs):
    landed = refs[:count]
    before_ref, total_ref, sums = refs[count], refs[-2], refs[-1]
    spectra_ref = refs[count + 1] if len(refs) > count + 3 else None
    step = pl.program_id(0)

    @pl.when(step == 0)
    def _():
        sums[...] = jnp.zeros_like(sums)

    data = jnp.concatenate([own_ref[0]] + [ref[...] for ref in landed], 0)
    weight = weight_ref[...]
    for group in range(GROUPS):
        wide = jnp.dot(band_ref[group], data, preferred_element_type=jnp.float32)
        spectra = wide.astype(jnp.bfloat16)
        if spectra_ref is not None:
            spectra_ref[group] = spectra
        weighted = (spectra.astype(jnp.float32) * weight).astype(jnp.bfloat16)
        sums[group] += lax.dot_general(
            weighted, spectra, (((1,), (1,)), ((), ())), preferred_element_type=jnp.float32
        )

    @pl.when(step == pl.num_programs(0) - 1)
    def _():
        rows = sums.shape[1]
        line = lax.broadcasted_iota(jnp.int32, (rows, rows), 0) % PER_GROUP
        column = lax.broadcasted_iota(jnp.int32, (rows, rows), 1) % PER_GROUP
        for group in range(GROUPS):
            kept = jnp.where(line == column, sums[group], 0.0)
            total_ref[group] = before_ref[group] + jnp.dot(
                fold_ref[...], kept, precision=lax.Precision.HIGHEST, preferred_element_type=jnp.float32
            )


def gather(me, band, fold, weights, own, landed, before, keep, comp, start, size, sub, tile):
    count = len(landed)
    devices = count + 1
    half = own.shape[1]
    rows = band.shape[1]
    whole = lambda shape: pl.BlockSpec(shape, lambda g, m: (0,) * len(shape))
    spot = lambda g, m: m[0] * (sub // tile) + start // tile + g
    return pl.pallas_call(
        functools.partial(gather_kernel, count),
        grid_spec=pltpu.PrefetchScalarGridSpec(
            num_scalar_prefetch=1,
            grid=(size // tile,),
            in_specs=[
                whole(band.shape),
                whole(fold.shape),
                pl.BlockSpec((1, tile), lambda g, m: (0, spot(g, m))),
                pl.BlockSpec((1, half, tile), lambda g, m: (comp, 0, spot(g, m))),
            ]
            + [pl.BlockSpec((half, tile), lambda g, m: (0, g))] * count
            + [whole(before.shape)],
            out_specs=[pl.BlockSpec((GROUPS, rows, tile), lambda g, m: (0, 0, g))] * keep + [whole(before.shape)],
            scratch_shapes=[pltpu.VMEM((GROUPS, rows, rows), jnp.float32)],
        ),
        out_shape=[
            jax.ShapeDtypeStruct((GROUPS, rows, size), jnp.bfloat16),
        ]
        * keep
        + [jax.ShapeDtypeStruct(before.shape, jnp.float32)],
        compiler_params=pltpu.CompilerParams(vmem_limit_bytes=vmem(devices)),
        cost_estimate=pl.CostEstimate(
            flops=2 * GROUPS * size * rows * (band.shape[2] + rows), bytes_accessed=2 * size * (2 * rows + 256), transcendentals=0
        ),
        name="gather",
    )(me, band, fold, weights, own, *landed, before)


def solve_kernel(blocks, me_ref, scale_ref, sums_ref, others_ref, start_ref, tile_ref, mix_ref, energy_ref):
    devices = mix_ref.shape[0]
    freqs = mix_ref.shape[1] // (2 * MODES)
    padded = sums_ref.shape[1] // 2
    gram_scale = scale_ref[0]
    factor = scale_ref[1]

    total = [sums_ref[g] + others_ref[g] for g in range(GROUPS)]

    def lanes(block, part):
        place = (2 * block + part) * PER_GROUP
        return jnp.concatenate([total[g][:, place : place + PER_GROUP] for g in range(GROUPS)], 1)

    real, imag = [], []
    for block in range(blocks):
        cosine, sine = lanes(block, 0), lanes(block, 1)
        real.append((cosine[:padded] + sine[padded:]) * gram_scale)
        imag.append((sine[:padded] - cosine[padded:]) * gram_scale)

    def apply(vec_re, vec_im):
        out_re = jnp.zeros((padded, NF), jnp.float32)
        out_im = out_re
        for block in range(blocks):
            at_re = vec_re[block : block + 1]
            at_im = vec_im[block : block + 1]
            out_re = out_re + (real[block] * at_re - imag[block] * at_im)
            out_im = out_im + (real[block] * at_im + imag[block] * at_re)
        return out_re, out_im

    def inner(value):
        return jnp.sum(value, axis=0, keepdims=True)

    vectors = [(start_ref[k], jnp.zeros((padded, NF), jnp.float32)) for k in range(MODES)]
    for sweep in range(SWEEPS):
        images = [apply(*vector) for vector in vectors]
        vectors = []
        for col_re, col_im in images:
            for prev_re, prev_im in vectors:
                inner_re = inner(prev_re * col_re + prev_im * col_im)
                inner_im = inner(prev_re * col_im - prev_im * col_re)
                col_re, col_im = (
                    col_re - (inner_re * prev_re - inner_im * prev_im),
                    col_im - (inner_re * prev_im + inner_im * prev_re),
                )
            length = jnp.sqrt(inner(col_re * col_re + col_im * col_im))
            vectors.append((col_re / length, col_im / length))
    for k, (vec_re, vec_im) in enumerate(vectors):
        applied_re, applied_im = apply(vec_re, vec_im)
        energy_ref[k : k + 1] = inner(vec_re * applied_re + vec_im * applied_im)

    straight, turned = [], []
    for vec_re, vec_im in vectors:
        straight += [vec_re * factor, vec_im * factor]
        turned += [-vec_im * factor, vec_re * factor]
    straight = jnp.concatenate(straight, 0).astype(jnp.bfloat16)
    turned = jnp.concatenate(turned, 0).astype(jnp.bfloat16)
    rows = tile_ref.shape[2]
    place = lax.broadcasted_iota(jnp.int32, (2 * MODES, padded, rows), 2)
    mine = place // (2 * PER_GROUP) == lax.broadcasted_iota(jnp.int32, (2 * MODES, padded, rows), 1)
    lane = lax.broadcasted_iota(jnp.int32, (2 * MODES, rows), 1)
    cosine = lane // PER_GROUP % 2 == 0
    me = me_ref[0]

    def spread(value, group):
        wide = jnp.dot(value, tile_ref[group], preferred_element_type=jnp.float32)
        wide = wide.reshape(2 * MODES, padded, rows)
        return jnp.sum(jnp.where(mine, wide, 0.0), axis=1)

    for group in range(GROUPS):
        both = jnp.where(cosine, spread(straight, group), spread(turned, group))
        for near in range(devices // GROUPS):
            device = group * (devices // GROUPS) + near
            pieces = [
                jnp.where(lane % PER_GROUP == near * freqs + f, both, 0.0) for f in range(freqs)
            ]
            mix_ref[jnp.bitwise_xor(me, device)] = jnp.concatenate(pieces, 0).astype(jnp.bfloat16)


def solve(me, scales, sums, others, start, tiles, devices):
    freqs = NF // devices
    rows = sums.shape[2]
    return pl.pallas_call(
        functools.partial(solve_kernel, devices - 1),
        in_specs=[pl.BlockSpec(memory_space=pltpu.SMEM)] * 2 + [pl.BlockSpec(memory_space=pltpu.VMEM)] * 4,
        out_specs=[pl.BlockSpec(memory_space=pltpu.VMEM)] * 2,
        out_shape=[
            jax.ShapeDtypeStruct((devices, freqs * MODES * 2, rows), jnp.bfloat16),
            jax.ShapeDtypeStruct((MODES, NF), jnp.float32),
        ],
        compiler_params=pltpu.CompilerParams(vmem_limit_bytes=vmem(devices)),
        name="solve",
    )(me, scales, sums, others, start, tiles)


def fetch_kernel(spectra_ref, after_ref, out_ref, sem):
    copy = pltpu.make_async_copy(spectra_ref, out_ref, sem)
    copy.start()
    copy.wait()


def fetch(spectra, after, devices):
    return pl.pallas_call(
        fetch_kernel,
        in_specs=[pl.BlockSpec(memory_space=pl.ANY)] * 2,
        out_specs=pl.BlockSpec(memory_space=pltpu.VMEM),
        out_shape=jax.ShapeDtypeStruct(spectra.shape, spectra.dtype),
        scratch_shapes=[pltpu.SemaphoreType.DMA(())],
        compiler_params=pltpu.CompilerParams(vmem_limit_bytes=vmem(devices)),
        name="fetch",
    )(spectra, after)


def modes_kernel(after, sides, me_ref, mix_ref, spectra_ref, *refs):
    outs = refs[after:]
    devices = mix_ref.shape[0]
    part = devices // GROUPS
    freqs = outs[0].shape[0]
    per = freqs * MODES * 2
    mine = me_ref[0] // part
    for number, side in enumerate(sides):
        mix = mix_ref[side * part : (side + 1) * part].reshape(part * per, mix_ref.shape[2])
        group = jnp.bitwise_xor(mine, side) if len(sides) > 1 else 0
        wide = jnp.dot(mix, spectra_ref[group], preferred_element_type=jnp.float32)
        for near in range(part):
            split_rows(wide[near * per : (near + 1) * per], outs[number * part + near])


def split_rows(wide, out):
    freqs, modes = out.shape[:2]
    for f in range(freqs):
        for k in range(modes):
            place = 2 * (f * modes + k)
            out[f, k] = wide[place : place + 2].astype(out.dtype)


def modes_of(me, mix, spectra, after, devices, sides, tile):
    freqs = NF // devices
    part = devices // GROUPS
    groups, rows, size = spectra.shape
    count = part * len(sides)
    if len(sides) == 1:
        source = pl.BlockSpec(
            (1, rows, tile), lambda g, m: (jnp.bitwise_xor(m[0] // part, sides[0]), 0, g)
        )
    else:
        source = pl.BlockSpec((groups, rows, tile), lambda g, m: (0, 0, g))
    made = pl.pallas_call(
        functools.partial(modes_kernel, len(after), sides),
        grid_spec=pltpu.PrefetchScalarGridSpec(
            num_scalar_prefetch=1,
            grid=(size // tile,),
            in_specs=[
                pl.BlockSpec(mix.shape, lambda g, m: (0, 0, 0)),
                source,
            ]
            + [pl.BlockSpec(memory_space=pl.ANY)] * len(after),
            out_specs=[pl.BlockSpec((freqs, MODES, 2, tile), lambda g, m: (0, 0, 0, g))] * count,
        ),
        out_shape=[jax.ShapeDtypeStruct((freqs, MODES, 2, size), jnp.bfloat16)] * count,
        compiler_params=pltpu.CompilerParams(vmem_limit_bytes=vmem(devices)),
        name="modes",
    )(me, mix, spectra, *after)
    return {side * part + near: made[n * part + near] for n, side in enumerate(sides) for near in range(part)}


def again_kernel(count, after, me_ref, band_ref, mix_ref, own_ref, *refs):
    landed, outs = refs[:count], refs[count + after :]
    devices = mix_ref.shape[0]
    part = devices // GROUPS
    freqs = outs[0].shape[0]
    per = freqs * MODES * 2
    mine = me_ref[0] // part
    data = jnp.concatenate([own_ref[0]] + [ref[...] for ref in landed], 0)
    for side in (0, 1):
        band = band_ref[jnp.bitwise_xor(mine, side)]
        spectra = jnp.dot(band, data, preferred_element_type=jnp.float32).astype(jnp.bfloat16)
        mix = mix_ref[side * part : (side + 1) * part].reshape(part * per, mix_ref.shape[2])
        wide = jnp.dot(mix, spectra, preferred_element_type=jnp.float32)
        for near in range(part):
            split_rows(wide[near * per : (near + 1) * per], outs[side * part + near])


def modes_again(me, band, mix, own, landed, after, devices, comp, start, size, sub, tile):
    freqs = NF // devices
    count = len(landed)
    half = own.shape[1]
    made = pl.pallas_call(
        functools.partial(again_kernel, count, len(after)),
        grid_spec=pltpu.PrefetchScalarGridSpec(
            num_scalar_prefetch=1,
            grid=(size // tile,),
            in_specs=[
                pl.BlockSpec(band.shape, lambda g, m: (0, 0, 0)),
                pl.BlockSpec(mix.shape, lambda g, m: (0, 0, 0)),
                pl.BlockSpec((1, half, tile), lambda g, m: (comp, 0, m[0] * (sub // tile) + start // tile + g)),
            ]
            + [pl.BlockSpec((half, tile), lambda g, m: (0, g))] * count
            + [pl.BlockSpec(memory_space=pl.ANY)] * len(after),
            out_specs=[pl.BlockSpec((freqs, MODES, 2, tile), lambda g, m: (0, 0, 0, g))] * devices,
        ),
        out_shape=[jax.ShapeDtypeStruct((freqs, MODES, 2, size), jnp.bfloat16)] * devices,
        compiler_params=pltpu.CompilerParams(vmem_limit_bytes=vmem(devices)),
        name="again",
    )(me, band, mix, own, *landed, *after)
    return dict(enumerate(made))


def place_kernel(spots, comp, sub, me_ref, *refs):
    count = len(spots)
    pieces, out_ref, sems = refs[:count], refs[-2], refs[-1]
    me = me_ref[0]
    copies = []
    for n, (turn, start) in enumerate(spots):
        there = pl.multiple_of(jnp.bitwise_xor(me, turn) * sub + start, 128)
        copies.append(
            pltpu.make_async_copy(
                pieces[n], out_ref.at[:, :, comp, :, pl.ds(there, pieces[n].shape[3])], sems.at[n]
            )
        )
    for copy in copies:
        copy.start()
    for copy in copies:
        copy.wait()


def place(me, pieces, out, devices, comp, sub, shape):
    arrays = [piece[0] for piece in pieces]
    count = len(pieces)
    more = [] if out is None else [out]
    return pl.pallas_call(
        functools.partial(place_kernel, [piece[1:] for piece in pieces], comp, sub),
        in_specs=[pl.BlockSpec(memory_space=pltpu.SMEM)]
        + [pl.BlockSpec(memory_space=pltpu.VMEM)] * count
        + [pl.BlockSpec(memory_space=pl.ANY)] * len(more),
        out_specs=pl.BlockSpec(memory_space=pl.ANY),
        out_shape=jax.ShapeDtypeStruct(shape, jnp.bfloat16),
        input_output_aliases={count + 1: 0} if more else {},
        scratch_shapes=[pltpu.SemaphoreType.DMA((count,))],
        compiler_params=pltpu.CompilerParams(vmem_limit_bytes=vmem(devices)),
        name="place",
    )(me, *arrays, *more)


def send(value, turn, devices):
    return lax.ppermute(value, "tm", [(d, d ^ turn) for d in range(devices)])


def exchange(pieces, devices):
    return [send(piece, turn, devices) for piece, turn in zip(pieces, turns(devices)[1:])]


def sum_over(value, axis, whole=True):
    count = lax.axis_size(axis)
    step = 1
    while step < (count if whole else count // 2):
        value = value + lax.ppermute(value, axis, [(d, d ^ step) for d in range(count)])
        step *= 2
    return value


def per_device(snapshots, cell_weights, freq_order):
    devices = lax.axis_size("tm")
    spaces = lax.axis_size("space")
    index = lax.axis_index("tm")
    me = index.astype(jnp.int32).reshape(1)
    half, comps, cells = snapshots.shape
    freqs = NF // devices
    blocks = devices - 1
    padded = -(-blocks // 8) * 8
    rows = blocks * 2 * PER_GROUP
    sub = cells // devices
    unit = sub // QUARTERS
    window = hann_window()
    energy_sum = jnp.sum(window * window)
    scales = jnp.stack([1.0 / (energy_sum * (comps * cells * spaces)), 1.0 / jnp.sqrt(energy_sum)])

    own = jnp.transpose(snapshots, (1, 0, 2))
    weights = cell_weights.reshape(1, cells)
    band = band_table(freq_order, index.astype(jnp.int32), devices)
    line = jnp.arange(rows, dtype=jnp.int32)
    target = line // PER_GROUP % 2 * padded + line // (2 * PER_GROUP)
    fold = (target[None, :] == jnp.arange(2 * padded, dtype=jnp.int32)[:, None]).astype(jnp.float32)
    freq_line = jnp.arange(NF, dtype=jnp.int32)
    tiles = jnp.stack(
        [freq_line[:, None] == g * PER_GROUP + line[None, :] % PER_GROUP for g in range(GROUPS)]
    ).astype(jnp.bfloat16)
    count_a = jnp.arange(padded, dtype=jnp.float32) + 1.0
    count_k = jnp.arange(MODES, dtype=jnp.float32) + 1.0
    start_table = jnp.cos(shift_rate * count_a[None, :] * count_k[:, None])
    start_table = jnp.where(jnp.arange(padded)[None, :] < blocks, start_table, 0.0)
    start_table = jnp.broadcast_to(start_table[:, :, None], (MODES, padded, NF))

    sums = jnp.zeros((GROUPS, 2 * padded, rows), jnp.float32)
    spectra = []
    history = []
    for comp, first, length in CHUNKS_IN:
        start, size = first * unit, length * unit
        order = turns(devices)[1:]
        cut = 0 if history else 1
        pieces = []
        for wanted in (order[:cut], order[cut:]):
            if wanted:
                pieces += pick(me, own, history[-2:-1], devices, wanted, comp, start, size, sub)
        landed = exchange(pieces, devices)
        keep = len(history) < len(CHUNKS_IN) - 1
        *made, sums = gather(me, band, fold, weights, own, landed, sums, keep, comp, start, size, sub, unit if keep else 4 * unit)
        spectra += made
        history.append(sums)
    sums = sum_over(sums, "space")
    ready = fetch(spectra[0], sums, devices)
    sums = sum_over(sums, "tm", False)
    others = lax.ppermute(sums, "tm", [(d, d ^ (devices // 2)) for d in range(devices)])
    mix, energies = solve(me, scales, sums, others, start_table, tiles, devices)
    placed = [None]
    shape = (freqs, MODES, comps, 2, cells)
    for chunk in CHUNKS_OUT:
        comp, first, length = CHUNKS_IN[chunk]
        after = [] if len(placed) < 3 else placed[-2:-1]
        pieces = []
        if chunk == 0:
            made = modes_of(me, mix, ready, after, devices, (1,), QUARTERS * unit)
            made.update(modes_of(me, mix, ready, after, devices, (0,), unit))
        elif chunk == len(CHUNKS_IN) - 1:
            made = modes_again(
                me, band, mix, own, landed, after, devices, comp, first * unit, length * unit, sub, unit
            )
        else:
            made = modes_of(me, mix, spectra[chunk], after, devices, (0, 1), unit)
        for turn in turns(devices):
            value = send(made[turn], turn, devices) if turn else made[turn]
            pieces.append((value, turn, first * unit))
        soon = pieces[:6] if chunk == CHUNKS_OUT[-1] else []
        done = place(me, soon, placed[-1], devices, comp, sub, shape) if soon else placed[-1]
        placed.append(place(me, pieces[len(soon) :], done, devices, comp, sub, shape))
    mine = lax.dynamic_slice_in_dim(energies, index * freqs, freqs, 1)
    return (jnp.transpose(mine), jnp.transpose(placed[-1], (0, 1, 3, 2, 4)))


def solution(mesh):
    return jax.shard_map(
        per_device,
        mesh=mesh,
        in_specs=(P("tm", None, "space"), P("space"), P()),
        out_specs=(P("tm", None), P("tm", None, None, None, "space")),
        check_vma=False,
    )
```
